32 devices in a mesh: tile: 8 (over z, x), row: 4 (over y, core).
Axes of the slice: x: 2, y: 2, z: 4, core: 2. Of those that a mesh axis runs over, the one named last changes fastest.
Arguments:
- amplitudes: float32 [576, 64, 256], P('tile'), may hold values from -6 to 6
- integrals: float32 [4, 512, 128, 256], P('row', 'tile'), may hold values from -0.125 to 0.125
- slot_ab: int32 [4, 512], P('row', 'tile'), may hold values from 0 to 17
- slot_cd: int32 [4, 512], P('row', 'tile'), may hold values from 0 to 575, as said below
- live_count: int32 [4, 8], P('row', 'tile'), may hold values from 1 to 64, as said below
- pair_list: int32 [64, 2], replicated, may hold values from 0 to 127, as said below
Outputs:
- symmetrized: float32 [64, 96, 96], P('tile', 'row')
The draws below stay inside these ranges and needn't reach their ends.
Inputs may be any that keep to these rules, and one draw needn't show every extreme that they name: `slot_cd`: slot s of row index r belongs to tile index k = s // 64; its cd tile is held in amplitudes by tile index k - 1, k or k + 1, taken cyclically over the tile axis (cd tile c is held by tile index c // 72). `live_count`: slots at or after a device's count are unused. In every row index some device uses all 64 slots. `pair_list`: the rows are distinct pairs (i, j) with i != j, and for every row the reversed pair (j, i) is also a row.
All inputs are finite; a program needn't handle non-finite values.
Results may differ from the reference program's by a relative error of at most 0.0003.
Values sent between devices are 32-bit elements; how exact they have to be, the bound alone decides.
A program may use at most 64 MiB of HBM per device.

```python
import jax
import jax.numpy as jnp
from jax import lax

NOCC = 128
TS = 16
ATS = 8
SLAB = 96
PAIRS = 64
KCAP = 64
TW = 256
ABW = 128
CDT = 576
CDT_DEV = 72
ABT_ROW = 18
SLOTS = 512
N_TILE = 8
N_ROW = 4


def draw_slot_cd(key, part):
    drawn = jax.random.randint(jax.random.fold_in(key, 11), (N_ROW, N_TILE * KCAP), 0, 3 * CDT_DEV)
    owners = jnp.arange(N_TILE * KCAP, dtype=jnp.int32) // KCAP
    owner_tile = (owners[None, :] + drawn // CDT_DEV + N_TILE - 1) % N_TILE
    return (owner_tile * CDT_DEV + drawn % CDT_DEV).astype(jnp.int32)


def draw_live_count(key, part):
    key_base, key_heavy, key_pick, key_top = jax.random.split(jax.random.fold_in(key, 23), 4)
    base_count = jax.random.randint(key_base, (N_ROW, N_TILE), max(1, KCAP // 8), KCAP // 2 + 1)
    heavy_count = jax.random.randint(key_heavy, (N_ROW, N_TILE), 3 * KCAP // 4, KCAP + 1)
    picked = jax.random.randint(key_pick, (N_ROW, N_TILE), 0, 8) == 0
    busiest = jax.random.randint(key_top, (N_ROW, 1), 0, N_TILE)
    counts = jnp.where(picked, heavy_count, base_count)
    counts = jnp.where(jnp.arange(N_TILE, dtype=jnp.int32)[None, :] == busiest, KCAP, counts)
    return counts.astype(jnp.int32)


def draw_pair_list(key, part):
    key_orbs, key_rows = jax.random.split(jax.random.fold_in(key, 37))
    shuffled = jax.random.permutation(key_orbs, NOCC)
    half_count = PAIRS // 2
    first_orb = shuffled[:half_count]
    second = shuffled[half_count:PAIRS]
    listed = jnp.concatenate([jnp.stack([first_orb, second], axis=1), jnp.stack([second, first_orb], axis=1)], axis=0)
    reorder = jax.random.permutation(key_rows, PAIRS)
    return jnp.take(listed, reorder, axis=0).astype(jnp.int32)


def with_ends(values, key, least, top_value):
    index_at = [jax.random.randint(jax.random.fold_in(key, axis), (), 0, length) for axis, length in enumerate(values.shape)]
    main_axis = values.shape.index(max(values.shape))
    neighbour = index_at[:main_axis] + [(index_at[main_axis] + 1) % values.shape[main_axis]] + index_at[main_axis + 1:]
    return values.at[tuple(index_at)].set(least).at[tuple(neighbour)].set(top_value)


def level_of(stream_key, extent, cuts, least, largest):
    factor_of = 1.0
    for axis_at, shards_of in cuts:
        steps = jax.random.uniform(jax.random.fold_in(jax.random.fold_in(stream_key, 6), axis_at), (shards_of,), jnp.float32, least / len(cuts), largest / len(cuts))
        factor_of = factor_of * jnp.repeat(jnp.exp(steps), extent[axis_at] // shards_of).reshape((-1,) + (1,) * (len(extent) - 1 - axis_at))
    return factor_of


def noise(stream_key, dims, scale, reach, shards=(), held_as=jnp.bfloat16):
    array = jax.random.normal(stream_key, dims, jnp.float32) * scale
    if len(shards) > 0:
        array = level_of(stream_key, dims, shards, -0.22, 0.18) * array
    return jnp.clip(array, min=-reach, max=reach).astype(held_as)


def setup_inputs(seed: int = 0) -> dict:
    key_of = jax.random.split(jax.random.key(seed), 7)
    amplitudes = noise(key_of[0], (CDT, PAIRS, TW), 1.0, 6.0, ((0, 8),), jnp.float32)
    integrals = noise(key_of[1], (N_ROW, SLOTS, ABW, TW), (TW * N_TILE * KCAP // (3 * ABT_ROW)) ** -0.5, 0.125, ((0, 4), (1, 8)), jnp.float32)
    slot_ab = with_ends(jax.random.randint(key_of[2], (N_ROW, SLOTS), 0, ABT_ROW), jax.random.fold_in(key_of[2], 1), 0, ABT_ROW - 1).astype(jnp.int32)
    slot_cd = draw_slot_cd(jax.random.fold_in(key_of[6], 71), 0)
    live_count = draw_live_count(jax.random.fold_in(key_of[6], 71), 0)
    pair_list = draw_pair_list(jax.random.fold_in(key_of[6], 71), 0)
    return {"amplitudes": amplitudes, "integrals": integrals, "slot_ab": slot_ab, "slot_cd": slot_cd, "live_count": live_count, "pair_list": pair_list}


def find_mirror(pair_list):
    first_orb = pair_list[:, 0]
    second = pair_list[:, 1]
    matches = (first_orb[:, None] == second[None, :]) & (second[:, None] == first_orb[None, :])
    columns = jnp.arange(pair_list.shape[0], dtype=jnp.int32)
    return jnp.sum(jnp.where(matches, columns[None, :], 0), axis=1).astype(jnp.int32)


def to_grid(totals, a_tiles, b_tiles):
    pair_count = totals.shape[1]
    shaped = totals.reshape(a_tiles, b_tiles, pair_count, ATS, TS)
    return jnp.transpose(shaped, (2, 0, 3, 1, 4)).reshape(pair_count, a_tiles * ATS, b_tiles * TS)


def reference(amplitudes, integrals, slot_ab, slot_cd, live_count, pair_list):
    highest = lax.Precision.HIGHEST
    a_tiles = SLAB // (N_ROW * ATS)
    b_tiles = SLAB // TS
    tiles_ab = a_tiles * b_tiles
    slices = []
    for row_index in range(N_ROW):
        def per_owner(totals, owner_index, row_index=row_index):
            first_slot = (owner_index * KCAP).astype(jnp.int32)
            cd_tiles = lax.dynamic_slice_in_dim(slot_cd[row_index], first_slot, KCAP)
            ab_tiles = lax.dynamic_slice_in_dim(slot_ab[row_index], first_slot, KCAP)
            blocks = lax.dynamic_slice_in_dim(integrals[row_index], first_slot, KCAP, 0)
            live_mask = (jnp.arange(KCAP, dtype=jnp.int32) < live_count[row_index, owner_index]).astype(jnp.float32)
            amp_tiles = jnp.take(amplitudes, cd_tiles, axis=0)
            products = jnp.einsum("spw,sbw->spb", amp_tiles, blocks, precision=highest)
            one_hot = (ab_tiles[:, None] == jnp.arange(tiles_ab, dtype=jnp.int32)[None, :]).astype(jnp.float32) * live_mask[:, None]
            return totals + jnp.einsum("se,spb->epb", one_hot, products, precision=highest), None

        start_totals = jnp.zeros((tiles_ab, PAIRS, ATS * TS), jnp.float32)
        totals, unused = lax.scan(per_owner, start_totals, jnp.arange(N_TILE, dtype=jnp.int32))
        slices.append(to_grid(totals, a_tiles, b_tiles))
    ladder = jnp.concatenate(slices, axis=1)
    mirrored = jnp.take(ladder, find_mirror(pair_list), axis=0)
    return ladder + jnp.transpose(mirrored, (0, 2, 1))
```

```python
import functools

import jax
import jax.numpy as jnp
from jax import lax
from jax.experimental import pallas as pl
from jax.experimental.pallas import tpu as pltpu
from jax.sharding import PartitionSpec as P

TS = 16
ATS = 8
SLAB = 96


def padded(x, sides, width):
    for axis, dim in sides:
        size, length = (lax.axis_size(axis), x.shape[dim])
        up = [(i, (i + 1) % size) for i in range(size)]
        down = [(j, i) for i, j in up]
        last = lax.slice_in_dim(x, length - width, length, axis=dim)
        first = lax.slice_in_dim(x, 0, width, axis=dim)
        before = lax.ppermute(last, axis, up)
        after = lax.ppermute(first, axis, down)
        x = jnp.concatenate([before, x, after], axis=dim)
    return x


def find_mirror(pair_list):
    first_orb = pair_list[:, 0]
    second = pair_list[:, 1]
    matches = (first_orb[:, None] == second[None, :]) & (second[:, None] == first_orb[None, :])
    columns = jnp.arange(pair_list.shape[0], dtype=jnp.int32)
    return jnp.sum(jnp.where(matches, columns[None, :], 0), axis=1)


def to_grid(totals, a_tiles, b_tiles):
    pair_count = totals.shape[1]
    shaped = totals.reshape(a_tiles, b_tiles, pair_count, ATS, TS)
    return jnp.transpose(shaped, (2, 0, 3, 1, 4)).reshape(pair_count, a_tiles * ATS, b_tiles * TS)


def shards(amplitudes, integrals, slot_ab, slot_cd, live_count, pair_list):
    highest = lax.Precision.HIGHEST
    tile_size = lax.axis_size("tile")
    row_size = lax.axis_size("row")
    tile_index = lax.axis_index("tile")
    shard_tiles = amplitudes.shape[0]
    pair_count = amplitudes.shape[1]
    extended = padded(amplitudes, (("tile", 0),), shard_tiles)
    blocks_all = integrals[0]
    ab_local = slot_ab[0]
    cd_global = slot_cd[0]
    owner_tile = cd_global // shard_tiles
    offset = (owner_tile - tile_index + 1 + tile_size) % tile_size
    ext_index = offset * shard_tiles + cd_global % shard_tiles
    live_total = live_count[0, 0]
    a_tiles = SLAB // (row_size * ATS)
    b_tiles = SLAB // TS
    tiles_ab = a_tiles * b_tiles
    block_width = integrals.shape[2]
    group_size = 8

    def block_step(block_index, totals):
        first_slot = block_index * group_size
        picked = lax.dynamic_slice_in_dim(ext_index, first_slot, group_size)
        ab_tiles = lax.dynamic_slice_in_dim(ab_local, first_slot, group_size)
        blocks = lax.dynamic_slice_in_dim(blocks_all, first_slot, group_size, 0)
        live_mask = (first_slot + jnp.arange(group_size, dtype=jnp.int32) < live_total).astype(
            jnp.float32
        )
        amp_tiles = jnp.take(extended, picked, axis=0)
        products = jnp.einsum(
            "spw,sbw->spb", amp_tiles, blocks, precision=highest, preferred_element_type=jnp.float32
        )
        one_hot = (ab_tiles[:, None] == jnp.arange(tiles_ab, dtype=jnp.int32)[None, :]).astype(
            jnp.float32
        ) * live_mask[:, None]
        return totals + jnp.einsum(
            "se,spb->epb", one_hot, products, precision=highest, preferred_element_type=jnp.float32
        )

    turn_count = (live_total + group_size - 1) // group_size
    start_totals = jnp.zeros((tiles_ab, pair_count, block_width), jnp.float32)
    totals = lax.fori_loop(0, turn_count, block_step, start_totals)
    whole_term = to_grid(totals, a_tiles, b_tiles)
    mirror = find_mirror(pair_list)
    reduced = lax.psum_scatter(whole_term, "tile", scatter_dimension=0, tiled=True)
    exchanged = lax.all_to_all(reduced, "row", split_axis=2, concat_axis=1, tiled=True)
    turned = jnp.transpose(exchanged, (0, 2, 1))
    everyone = lax.all_gather(turned, "tile", axis=0, tiled=True)
    local_pairs = reduced.shape[0]
    wanted = lax.dynamic_slice_in_dim(mirror, tile_index * local_pairs, local_pairs)
    return reduced + jnp.take(everyone, wanted, axis=0)


MESH = pl.DeviceIdType.MESH
CHUNK = 2
GROUP = 4
DEPTH = 3


def place():
    k = lax.axis_index("tile")
    r = lax.axis_index("row")
    return k, r, k // 2, k % 2


def greet(devices):
    barrier = pltpu.get_barrier_semaphore()
    for device in devices:
        pl.semaphore_signal(barrier, inc=1, device_id=device, device_id_type=MESH)
    pl.semaphore_wait(barrier, len(devices))


def halo_kernel(tiles, amp, halo, send, rx, rz, ry, rc):
    k, r, z, x = place()
    y, core = r // 2, r % 2
    sixth = tiles // 6
    half = sixth // CHUNK
    count = 2 * half
    other_x = (z * 2 + 1 - x, r)
    up = ((z + 1) % 4 * 2 + x, r)
    down = ((z + 3) % 4 * 2 + x, r)
    next_z = (jnp.where(x == 0, up[0], down[0]), r)
    other_y = (k, (1 - y) * 2 + core)
    other_core = (k, y * 2 + 1 - core)
    greet((other_x, up, down, other_y, other_core))

    def first_of(yy, cc, j):
        own = (yy * 2 + cc) * sixth + j * CHUNK
        both = (4 + cc) * sixth + (j - half) * CHUNK
        return own if j < half else both

    def remote(src, dst, sent, received, device):
        return pltpu.make_async_remote_copy(
            src_ref=src, dst_ref=dst, send_sem=sent, recv_sem=received, device_id=device, device_id_type=MESH
        )

    def at(side, first):
        return halo.at[side, pl.ds(first, CHUNK)]

    def copy_x(j):
        first = first_of(y, core, j)
        return remote(amp.at[pl.ds(first, CHUNK)], at(0, first), send.at[0, j], rx.at[j], other_x)

    def copy_z(j):
        first = first_of(y, core, j)
        return remote(at(0, first), at(1, first), send.at[1, j], rz.at[j], next_z)

    def copy_y(side, j):
        first = first_of(y, core, j)
        return remote(at(side, first), at(side, first), send.at[2 + side, j], ry.at[side, j], other_y)

    def copy_c(side, j):
        first = first_of(y, core, j) if j < count else first_of(1 - y, core, j - count)
        return remote(at(side, first), at(side, first), send.at[4 + side, j], rc.at[side, j], other_core)

    sends = []

    def go(copy):
        copy.start()
        sends.append(copy)

    for j in range(count):
        go(copy_x(j))
    lag = 1
    for i in range(count + 3 * lag):
        if i < count:
            copy_x(i).wait_recv()
            go(copy_z(i))
            if i < half:
                go(copy_y(0, i))
            go(copy_c(0, i))
        j = i - lag
        if 0 <= j < count:
            copy_z(j).wait_recv()
            if j < half:
                go(copy_y(1, j))
            go(copy_c(1, j))
        j = i - 2 * lag
        if 0 <= j < half:
            copy_y(0, j).wait_recv()
            go(copy_c(0, count + j))
        j = i - 3 * lag
        if 0 <= j < half:
            copy_y(1, j).wait_recv()
            go(copy_c(1, count + j))
    for j in range(count + half):
        for side in range(2):
            copy_c(side, j).wait_recv()
    for copy in sends:
        copy.wait_send()


def halo_of(amplitudes):
    tiles = amplitudes.shape[0]
    count = tiles // 3 // CHUNK
    return pl.pallas_call(
        functools.partial(halo_kernel, tiles),
        out_shape=jax.ShapeDtypeStruct((2,) + amplitudes.shape, jnp.float32),
        in_specs=[pl.BlockSpec(memory_space=pl.ANY)],
        out_specs=pl.BlockSpec(memory_space=pl.ANY),
        scratch_shapes=[
            pltpu.SemaphoreType.DMA((6, count + count // 2)),
            pltpu.SemaphoreType.DMA((count,)),
            pltpu.SemaphoreType.DMA((count,)),
            pltpu.SemaphoreType.DMA((2, count // 2)),
            pltpu.SemaphoreType.DMA((2, count + count // 2)),
        ],
        compiler_params=pltpu.CompilerParams(collective_id=0, has_side_effects=True),
    )(amplitudes)


def split(v):
    high = v.astype(jnp.bfloat16)
    low = (v - high.astype(jnp.float32)).astype(jnp.bfloat16)
    return jnp.concatenate([high, low], axis=0)


def slots_kernel(amp, halo, blocks, ab, cd, live, pairs, out, abuf, bbuf, asem, bsem, table):
    k = lax.axis_index("tile")
    tiles = amp.shape[0]
    pair_count = amp.shape[1]
    width = blocks.shape[1]
    groups = (live[0, 0] + GROUP - 1) // GROUP

    def copies(s, slot, from_amp, from_halo):
        c = cd[0, s]
        owner = c // tiles
        local = c - owner * tiles
        side = jnp.where(owner == k // 2 * 2 + 1 - k % 2, 0, 1)
        if from_amp:
            return pltpu.make_async_copy(amp.at[local], abuf.at[slot], asem.at[slot])
        if from_halo:
            return pltpu.make_async_copy(halo.at[side, local], abuf.at[slot], asem.at[slot])
        return pltpu.make_async_copy(blocks.at[s], bbuf.at[slot], bsem.at[slot])

    def fetch(g):
        @pl.when(g < groups)
        def _():
            for i in range(GROUP):
                s = g * GROUP + i
                slot = g % DEPTH * GROUP + i
                own = cd[0, s] // tiles == k
                pl.when(own)(lambda: copies(s, slot, True, False).start())
                pl.when(jnp.logical_not(own))(lambda: copies(s, slot, False, True).start())
                copies(s, slot, False, False).start()

    for g in range(DEPTH - 1):
        fetch(g)
    out[...] = jnp.zeros_like(out)

    def note(p, carry):
        table[pairs[p, 0] * 128 + pairs[p, 1]] = p
        return carry

    lax.fori_loop(0, pair_count, note, 0)

    def step(g, carry):
        fetch(g + DEPTH - 1)
        base = g % DEPTH * GROUP
        for i in range(GROUP):
            slot = base + i
            pltpu.make_async_copy(amp.at[0], abuf.at[slot], asem.at[slot]).wait()
            pltpu.make_async_copy(blocks.at[0], bbuf.at[slot], bsem.at[slot]).wait()
        terms = []
        for i in range(GROUP):
            left = split(abuf[base + i])
            right = split(bbuf[base + i])
            full = lax.dot_general(
                left, right, (((1,), (1,)), ((), ())), preferred_element_type=jnp.float32
            )
            top, low = full[:pair_count], full[pair_count:]
            terms.append(top[:, :width] + (top[:, width:] + (low[:, :width] + low[:, width:])))
        for i in range(GROUP):
            s = g * GROUP + i
            term = jnp.where(s < live[0, 0], terms[i], 0.0).reshape(out.shape[0], out.shape[3], width)
            e = ab[0, s]
            out[:, 0, e] += term
        return carry

    lax.fori_loop(0, groups, step, 0)

    def turn(p, carry):
        m = table[pairs[p, 1] * 128 + pairs[p, 0]]
        out[p // 8, 1, :, pl.ds(p % 8, 1), :] = out[m // 8, 0, :, pl.ds(m % 8, 1), :]
        return carry

    lax.fori_loop(0, pair_count, turn, 0)


def slot_sums(amplitudes, halo, blocks, ab, cd, live, pair_list, tiles_ab):
    pair_count, depth = amplitudes.shape[1:]
    width = blocks.shape[1]
    anywhere = pl.BlockSpec(memory_space=pl.ANY)
    scalars = pl.BlockSpec(memory_space=pltpu.SMEM)
    return pl.pallas_call(
        slots_kernel,
        out_shape=jax.ShapeDtypeStruct((pair_count // 8, 2, tiles_ab, 8, width), jnp.float32),
        in_specs=[anywhere] * 3 + [scalars] * 4,
        out_specs=pl.BlockSpec(memory_space=pltpu.VMEM),
        scratch_shapes=[
            pltpu.VMEM((DEPTH * GROUP, pair_count, depth), jnp.float32),
            pltpu.VMEM((DEPTH * GROUP, width, depth), jnp.float32),
            pltpu.SemaphoreType.DMA((DEPTH * GROUP,)),
            pltpu.SemaphoreType.DMA((DEPTH * GROUP,)),
            pltpu.SMEM((128 * 128,), jnp.int32),
        ],
        compiler_params=pltpu.CompilerParams(vmem_limit_bytes=32 * 1024 * 1024),
    )(amplitudes, halo, blocks, ab, cd, live, pair_list)


def sum_kernel(sums, ladder, turned, bx, sz, bz, mine, send_x, recv_x, send_z, recv_z, send_r, recv_r):
    k, r, z, x = place()
    other_x = (z * 2 + 1 - x, r)
    zs = [((z + i) % 4 * 2 + x, r) for i in range(1, 4)]
    rows = [(k, (r + i) % 4) for i in range(1, 4)]
    greet([other_x] + zs + rows)

    def remote(src, dst, sent, received, device):
        return pltpu.make_async_remote_copy(
            src_ref=src, dst_ref=dst, send_sem=sent, recv_sem=received, device_id=device, device_id_type=MESH
        )

    order = (2, 1, 3, 0)
    over_x = [remote(sums.at[(z + i) % 4 * 2 + 1 - x], bx.at[i], send_x.at[i], recv_x.at[i], other_x) for i in range(4)]
    over_z = [None] + [remote(sz.at[i], bz.at[i], send_z.at[i], recv_z.at[i], zs[i - 1]) for i in range(1, 4)]
    for i in order:
        over_x[i].start()
    for i in order:
        over_x[i].wait_recv()
        total = bx[i] + sums[(z + i) % 4 * 2 + x]
        if i > 0:
            sz[i] = total
            over_z[i].start()
        else:
            mine[...] = total
    for i in (1, 3, 2):
        over_z[i].wait_recv()
    total = mine[...] + bz[1] + bz[2] + bz[3]
    ladder[...] = total[0].reshape(ladder.shape)
    mine[...] = total
    parts = mine.at[1]

    def over_row(i):
        first = (r + i) % 4 * 3 // 2
        return [
            remote(
                parts.at[pl.ds(t * 6 + first, 2)], turned.at[r, t], send_r.at[i, t], recv_r.at[i, t], rows[i - 1]
            )
            for t in range(3)
        ]

    copies = [c for i in range(1, 4) for c in over_row(i)]
    for c in copies:
        c.start()
    own = r * 3 // 2
    for t in range(3):
        turned[r, t] = mine[1, pl.ds(t * 6 + own, 2)]
    for i in range(1, 4):
        source = (r + 4 - i) % 4
        for t in range(3):
            remote(
                parts.at[pl.ds(0, 2)], turned.at[source, t], send_r.at[i, t], recv_r.at[i, t], rows[i - 1]
            ).wait_recv()
    for c in copies + over_x + over_z[1:]:
        c.wait_send()


def sum_over_tile(sums):
    chunk = sums.shape[1:]
    vmem = pl.BlockSpec(memory_space=pltpu.VMEM)
    dma = pltpu.SemaphoreType.DMA
    return pl.pallas_call(
        sum_kernel,
        out_shape=(
            jax.ShapeDtypeStruct((3, 6) + chunk[2:], jnp.float32),
            jax.ShapeDtypeStruct((4, 3, 2) + chunk[2:], jnp.float32),
        ),
        in_specs=[vmem],
        out_specs=(vmem, vmem),
        scratch_shapes=[
            pltpu.VMEM((4,) + chunk, jnp.float32),
            pltpu.VMEM((4,) + chunk, jnp.float32),
            pltpu.VMEM((4,) + chunk, jnp.float32),
            pltpu.VMEM(chunk, jnp.float32),
            dma((4,)), dma((4,)), dma((4,)), dma((4,)), dma((4, 3)), dma((4, 3)),
        ],
        compiler_params=pltpu.CompilerParams(
            collective_id=1, has_side_effects=True, vmem_limit_bytes=32 * 1024 * 1024
        ),
    )(sums)


def shards_8x4(amplitudes, integrals, slot_ab, slot_cd, live_count, pair_list):
    halo = halo_of(amplitudes)
    sums = slot_sums(amplitudes, halo, integrals[0], slot_ab, slot_cd, live_count, pair_list, 18)
    ladder, turned = sum_over_tile(sums)
    local_pairs = ladder.shape[2]
    grid = jnp.transpose(ladder.reshape(3, 6, local_pairs, ATS, TS), (2, 0, 3, 1, 4)).reshape(local_pairs, 24, SLAB)
    other = turned.reshape(4, 3, 2, local_pairs, ATS, TS)
    other = jnp.transpose(other, (3, 2, 5, 0, 1, 4)).reshape(local_pairs, 2 * TS, SLAB)
    shift = lax.axis_index("row") % 2 * 8
    return grid + lax.dynamic_slice_in_dim(other, shift, 24, axis=1)


def solution(mesh):
    fast = mesh.shape["tile"] == 8 and mesh.shape["row"] == 4
    return jax.shard_map(
        shards_8x4 if fast else shards,
        mesh=mesh,
        in_specs=(
            P("tile", None, None),
            P("row", "tile", None, None),
            P("row", "tile"),
            P("row", "tile"),
            P("row", "tile"),
            P(),
        ),
        out_specs=P("tile", "row", None),
        check_vma=False,
    )
```

```python
import functools

import jax
import jax.numpy as jnp
from jax import lax
from jax.experimental import pallas as pl
from jax.experimental.pallas import tpu as pltpu
from jax.sharding import PartitionSpec as P

TS = 16
ATS = 8
SLAB = 96


def padded(x, sides, width):
    for axis, dim in sides:
        size, length = (lax.axis_size(axis), x.shape[dim])
        up = [(i, (i + 1) % size) for i in range(size)]
        down = [(j, i) for i, j in up]
        last = lax.slice_in_dim(x, length - width, length, axis=dim)
        first = lax.slice_in_dim(x, 0, width, axis=dim)
        before = lax.ppermute(last, axis, up)
        after = lax.ppermute(first, axis, down)
        x = jnp.concatenate([before, x, after], axis=dim)
    return x


def find_mirror(pair_list):
    first_orb = pair_list[:, 0]
    second = pair_list[:, 1]
    matches = (first_orb[:, None] == second[None, :]) & (second[:, None] == first_orb[None, :])
    columns = jnp.arange(pair_list.shape[0], dtype=jnp.int32)
    return jnp.sum(jnp.where(matches, columns[None, :], 0), axis=1)


def to_grid(totals, a_tiles, b_tiles):
    pair_count = totals.shape[1]
    shaped = totals.reshape(a_tiles, b_tiles, pair_count, ATS, TS)
    return jnp.transpose(shaped, (2, 0, 3, 1, 4)).reshape(pair_count, a_tiles * ATS, b_tiles * TS)


def shards(amplitudes, integrals, slot_ab, slot_cd, live_count, pair_list):
    highest = lax.Precision.HIGHEST
    tile_size = lax.axis_size("tile")
    row_size = lax.axis_size("row")
    tile_index = lax.axis_index("tile")
    shard_tiles = amplitudes.shape[0]
    pair_count = amplitudes.shape[1]
    extended = padded(amplitudes, (("tile", 0),), shard_tiles)
    blocks_all = integrals[0]
    ab_local = slot_ab[0]
    cd_global = slot_cd[0]
    owner_tile = cd_global // shard_tiles
    offset = (owner_tile - tile_index + 1 + tile_size) % tile_size
    ext_index = offset * shard_tiles + cd_global % shard_tiles
    live_total = live_count[0, 0]
    a_tiles = SLAB // (row_size * ATS)
    b_tiles = SLAB // TS
    tiles_ab = a_tiles * b_tiles
    block_width = integrals.shape[2]
    group_size = 8

    def block_step(block_index, totals):
        first_slot = block_index * group_size
        picked = lax.dynamic_slice_in_dim(ext_index, first_slot, group_size)
        ab_tiles = lax.dynamic_slice_in_dim(ab_local, first_slot, group_size)
        blocks = lax.dynamic_slice_in_dim(blocks_all, first_slot, group_size, 0)
        live_mask = (first_slot + jnp.arange(group_size, dtype=jnp.int32) < live_total).astype(
            jnp.float32
        )
        amp_tiles = jnp.take(extended, picked, axis=0)
        products = jnp.einsum(
            "spw,sbw->spb", amp_tiles, blocks, precision=highest, preferred_element_type=jnp.float32
        )
        one_hot = (ab_tiles[:, None] == jnp.arange(tiles_ab, dtype=jnp.int32)[None, :]).astype(
            jnp.float32
        ) * live_mask[:, None]
        return totals + jnp.einsum(
            "se,spb->epb", one_hot, products, precision=highest, preferred_element_type=jnp.float32
        )

    turn_count = (live_total + group_size - 1) // group_size
    start_totals = jnp.zeros((tiles_ab, pair_count, block_width), jnp.float32)
    totals = lax.fori_loop(0, turn_count, block_step, start_totals)
    whole_term = to_grid(totals, a_tiles, b_tiles)
    mirror = find_mirror(pair_list)
    reduced = lax.psum_scatter(whole_term, "tile", scatter_dimension=0, tiled=True)
    exchanged = lax.all_to_all(reduced, "row", split_axis=2, concat_axis=1, tiled=True)
    turned = jnp.transpose(exchanged, (0, 2, 1))
    everyone = lax.all_gather(turned, "tile", axis=0, tiled=True)
    local_pairs = reduced.shape[0]
    wanted = lax.dynamic_slice_in_dim(mirror, tile_index * local_pairs, local_pairs)
    return reduced + jnp.take(everyone, wanted, axis=0)


MESH = pl.DeviceIdType.MESH
CHUNK = 2
WINDOW = 2
GROUP = 8
AHEAD = 2
VMEM_BYTES = 56 * 1024 * 1024


def place():
    k = lax.axis_index("tile")
    r = lax.axis_index("row")
    return k, r, k // 2, k % 2


def greet(devices):
    barrier = pltpu.get_barrier_semaphore()
    for device in devices:
        pl.semaphore_signal(barrier, inc=1, device_id=device, device_id_type=MESH)
    pl.semaphore_wait(barrier, len(devices))


def halo_kernel(tiles, amp, halo, send, rx, rz, ry, rc, own_sem):
    k, r, z, x = place()
    y, core = r // 2, r % 2
    sixth = tiles // 6
    half = sixth // CHUNK
    count = 2 * half
    other_x = (z * 2 + 1 - x, r)
    up = ((z + 1) % 4 * 2 + x, r)
    down = ((z + 3) % 4 * 2 + x, r)
    next_z = (jnp.where(x == 0, up[0], down[0]), r)
    other_y = (k, (1 - y) * 2 + core)
    other_core = (k, y * 2 + 1 - core)
    greet((other_x, up, down, other_y, other_core))

    def first_of(yy, cc, j):
        own = (yy * 2 + cc) * sixth + j * CHUNK
        both = (4 + cc) * sixth + (j - half) * CHUNK
        return own if j < half else both

    def remote(src, dst, sent, received, device):
        return pltpu.make_async_remote_copy(
            src_ref=src, dst_ref=dst, send_sem=sent, recv_sem=received, device_id=device, device_id_type=MESH
        )

    def at(side, first):
        return halo.at[pl.ds(side * tiles + first, CHUNK)]

    def copy_x(j):
        first = first_of(y, core, j)
        return remote(amp.at[pl.ds(first, CHUNK)], at(0, first), send.at[0, j], rx.at[j], other_x)

    def copy_z(j):
        first = first_of(y, core, j)
        return remote(at(0, first), at(1, first), send.at[1, j], rz.at[j], next_z)

    def copy_y(side, j):
        first = first_of(y, core, j)
        return remote(at(side, first), at(side, first), send.at[2 + side, j], ry.at[side, j], other_y)

    def copy_c(side, j):
        first = first_of(y, core, j) if j < count else first_of(1 - y, core, j - count)
        return remote(at(side, first), at(side, first), send.at[4 + side, j], rc.at[side, j], other_core)

    sends = []

    def go(copy):
        copy.start()
        sends.append(copy)

    for j in range(WINDOW):
        go(copy_x(j))
    own = pltpu.make_async_copy(amp, halo.at[pl.ds(2 * tiles, tiles)], own_sem)
    own.start()
    lag = 1
    for i in range(count + 3 * lag):
        if i < count:
            copy_x(i).wait_recv()
            if i + WINDOW < count:
                go(copy_x(i + WINDOW))
            go(copy_z(i))
            if i < half:
                go(copy_y(0, i))
            go(copy_c(0, i))
        j = i - lag
        if 0 <= j < count:
            copy_z(j).wait_recv()
            if j < half:
                go(copy_y(1, j))
            go(copy_c(1, j))
        j = i - 2 * lag
        if 0 <= j < half:
            copy_y(0, j).wait_recv()
            go(copy_c(0, count + j))
        j = i - 3 * lag
        if 0 <= j < half:
            copy_y(1, j).wait_recv()
            go(copy_c(1, count + j))
    for j in range(count + half):
        for side in range(2):
            copy_c(side, j).wait_recv()
    for copy in sends:
        copy.wait_send()
    own.wait()


def halo_of(amplitudes):
    tiles = amplitudes.shape[0]
    count = tiles // 3 // CHUNK
    return pl.pallas_call(
        functools.partial(halo_kernel, tiles),
        out_shape=jax.ShapeDtypeStruct((3 * tiles,) + amplitudes.shape[1:], jnp.float32),
        in_specs=[pl.BlockSpec(memory_space=pl.ANY)],
        out_specs=pl.BlockSpec(memory_space=pl.ANY),
        scratch_shapes=[
            pltpu.SemaphoreType.DMA((6, count + count // 2)),
            pltpu.SemaphoreType.DMA((count,)),
            pltpu.SemaphoreType.DMA((count,)),
            pltpu.SemaphoreType.DMA((2, count // 2)),
            pltpu.SemaphoreType.DMA((2, count + count // 2)),
            pltpu.SemaphoreType.DMA,
        ],
        compiler_params=pltpu.CompilerParams(
            collective_id=0, has_side_effects=True, vmem_limit_bytes=VMEM_BYTES
        ),
    )(amplitudes)


def split(v):
    high = v.astype(jnp.bfloat16)
    low = (v - high.astype(jnp.float32)).astype(jnp.bfloat16)
    return jnp.concatenate([high, low], axis=0)


def slots_kernel(halo, blocks, ab, cd, live, pairs, out, abuf, bbuf, asem, bsem, table):
    k = lax.axis_index("tile")
    tiles = halo.shape[0] // 3
    pair_count = halo.shape[1]
    width = blocks.shape[1]
    groups = (live[0, 0] + GROUP - 1) // GROUP
    x = k % 2
    other_x = k + 1 - 2 * x
    next_z = lax.rem(k + 7 + 2 * x, 8)

    def block_copy(g):
        return pltpu.make_async_copy(
            blocks.at[pl.ds(g * GROUP, GROUP)], bbuf.at[pl.ds(g * GROUP, GROUP)], bsem.at[g]
        )

    def fetch(g):
        for i in range(GROUP):
            s = g * GROUP + i
            c = cd[0, s]
            mine = (c >= k * tiles) & (c < (k + 1) * tiles)
            beside = (c >= other_x * tiles) & (c < (other_x + 1) * tiles)
            shift = jnp.where(mine, 2 - k, jnp.where(beside, -other_x, 1 - next_z))
            pltpu.make_async_copy(halo.at[c + shift * tiles], abuf.at[s], asem.at[g]).start()

    def start_blocks(g, carry):
        block_copy(g).start()
        return carry

    block_copy(0).start()
    fetch(0)
    lax.fori_loop(1, groups, start_blocks, 0)
    for g in range(1, AHEAD):
        pl.when(g < groups)(functools.partial(fetch, g))
    out[...] = jnp.zeros_like(out)

    def note(p, carry):
        table[pairs[p, 0] * 128 + pairs[p, 1]] = p
        return carry

    lax.fori_loop(0, pair_count, note, 0)

    def step(g, carry):
        base = g * GROUP
        pl.when(g + AHEAD < groups)(lambda: fetch(g + AHEAD))
        pltpu.make_async_copy(
            halo.at[pl.ds(0, GROUP)], abuf.at[pl.ds(base, GROUP)], asem.at[g]
        ).wait()
        block_copy(g).wait()
        terms = []
        for i in range(GROUP):
            left = split(abuf[base + i])
            right = split(bbuf[base + i])
            full = lax.dot_general(
                left, right, (((1,), (1,)), ((), ())), preferred_element_type=jnp.float32
            )
            top, low = full[:pair_count], full[pair_count:]
            terms.append(top[:, :width] + (top[:, width:] + (low[:, :width] + low[:, width:])))
        for i in range(GROUP):
            s = g * GROUP + i
            term = jnp.where(s < live[0, 0], terms[i], 0.0).reshape(out.shape[0], out.shape[3], width)
            e = ab[0, s]
            out[:, 0, e] += term
        return carry

    lax.fori_loop(0, groups, step, 0)

    def turn(p, carry):
        m = table[pairs[p, 1] * 128 + pairs[p, 0]]
        out[p // 8, 1, :, pl.ds(p % 8, 1), :] = out[m // 8, 0, :, pl.ds(m % 8, 1), :]
        return carry

    lax.fori_loop(0, pair_count, turn, 0)


def slot_sums(halo, blocks, ab, cd, live, pair_list, tiles_ab):
    pair_count, depth = halo.shape[1:]
    slots, width = blocks.shape[:2]
    anywhere = pl.BlockSpec(memory_space=pl.ANY)
    scalars = pl.BlockSpec(memory_space=pltpu.SMEM)
    return pl.pallas_call(
        slots_kernel,
        out_shape=jax.ShapeDtypeStruct((pair_count // 8, 2, tiles_ab, 8, width), jnp.float32),
        in_specs=[anywhere] * 2 + [scalars] * 4,
        out_specs=pl.BlockSpec(memory_space=pltpu.VMEM),
        scratch_shapes=[
            pltpu.VMEM((slots, pair_count, depth), jnp.float32),
            pltpu.VMEM((slots, width, depth), jnp.float32),
            pltpu.SemaphoreType.DMA((slots // GROUP,)),
            pltpu.SemaphoreType.DMA((slots // GROUP,)),
            pltpu.SMEM((128 * 128,), jnp.int32),
        ],
        compiler_params=pltpu.CompilerParams(vmem_limit_bytes=VMEM_BYTES),
    )(halo, blocks, ab, cd, live, pair_list)


def sum_kernel(sums, ladder, turned, bx, sz, bz, mine, send_x, recv_x, send_z, recv_z, send_r, recv_r):
    k, r, z, x = place()
    other_x = (z * 2 + 1 - x, r)
    zs = [((z + i) % 4 * 2 + x, r) for i in range(1, 4)]
    rows = [(k, (r + i) % 4) for i in range(1, 4)]
    greet([other_x] + zs + rows)

    def remote(src, dst, sent, received, device):
        return pltpu.make_async_remote_copy(
            src_ref=src, dst_ref=dst, send_sem=sent, recv_sem=received, device_id=device, device_id_type=MESH
        )

    steps = [(i, h) for i in (2, 1, 3, 0) for h in range(2)]
    over_x = {
        (i, h): remote(
            sums.at[(z + i) % 4 * 2 + 1 - x, h], bx.at[i, h], send_x.at[i, h], recv_x.at[i, h], other_x
        )
        for i, h in steps
    }
    over_z = {
        (i, h): remote(sz.at[i, h], bz.at[i, h], send_z.at[i, h], recv_z.at[i, h], zs[i - 1])
        for i, h in steps if i > 0
    }
    for step in steps[:WINDOW]:
        over_x[step].start()
    for j, (i, h) in enumerate(steps):
        over_x[i, h].wait_recv()
        if j + WINDOW < len(steps):
            over_x[steps[j + WINDOW]].start()
        total = bx[i, h] + sums[(z + i) % 4 * 2 + x, h]
        if i > 0:
            sz[i, h] = total
            over_z[i, h].start()
        else:
            mine[h] = total
    for i in (1, 3, 2):
        for h in range(2):
            over_z[i, h].wait_recv()
    total = mine[...] + bz[1] + bz[2] + bz[3]
    ladder[...] = total[0].reshape(ladder.shape)
    mine[...] = total
    parts = mine.at[1]

    def over_row(i):
        first = (r + i) % 4 * 3 // 2
        return [
            remote(
                parts.at[pl.ds(t * 6 + first, 2)], turned.at[r, t], send_r.at[i, t], recv_r.at[i, t], rows[i - 1]
            )
            for t in range(3)
        ]

    copies = [c for i in range(1, 4) for c in over_row(i)]
    for c in copies:
        c.start()
    own = r * 3 // 2
    for t in range(3):
        turned[r, t] = mine[1, pl.ds(t * 6 + own, 2)]
    for i in range(1, 4):
        source = (r + 4 - i) % 4
        for t in range(3):
            remote(
                parts.at[pl.ds(0, 2)], turned.at[source, t], send_r.at[i, t], recv_r.at[i, t], rows[i - 1]
            ).wait_recv()
    for c in copies + list(over_x.values()) + list(over_z.values()):
        c.wait_send()


def sum_over_tile(sums):
    chunk = sums.shape[1:]
    vmem = pl.BlockSpec(memory_space=pltpu.VMEM)
    dma = pltpu.SemaphoreType.DMA
    return pl.pallas_call(
        sum_kernel,
        out_shape=(
            jax.ShapeDtypeStruct((3, 6) + chunk[2:], jnp.float32),
            jax.ShapeDtypeStruct((4, 3, 2) + chunk[2:], jnp.float32),
        ),
        in_specs=[vmem],
        out_specs=(vmem, vmem),
        scratch_shapes=[
            pltpu.VMEM((4,) + chunk, jnp.float32),
            pltpu.VMEM((4,) + chunk, jnp.float32),
            pltpu.VMEM((4,) + chunk, jnp.float32),
            pltpu.VMEM(chunk, jnp.float32),
            dma((4, 2)), dma((4, 2)), dma((4, 2)), dma((4, 2)), dma((4, 3)), dma((4, 3)),
        ],
        compiler_params=pltpu.CompilerParams(
            collective_id=1, has_side_effects=True, vmem_limit_bytes=VMEM_BYTES
        ),
    )(sums)


def shards_8x4(amplitudes, integrals, slot_ab, slot_cd, live_count, pair_list):
    halo = halo_of(amplitudes)
    sums = slot_sums(halo, integrals[0], slot_ab, slot_cd, live_count, pair_list, 18)
    ladder, turned = sum_over_tile(sums)
    local_pairs = ladder.shape[2]
    grid = jnp.transpose(ladder.reshape(3, 6, local_pairs, ATS, TS), (2, 0, 3, 1, 4)).reshape(local_pairs, 24, SLAB)
    other = turned.reshape(4, 3, 2, local_pairs, ATS, TS)
    other = jnp.transpose(other, (3, 2, 5, 0, 1, 4)).reshape(local_pairs, 2 * TS, SLAB)
    shift = lax.axis_index("row") % 2 * 8
    return grid + lax.dynamic_slice_in_dim(other, shift, 24, axis=1)


def solution(mesh):
    fast = mesh.shape["tile"] == 8 and mesh.shape["row"] == 4
    return jax.shard_map(
        shards_8x4 if fast else shards,
        mesh=mesh,
        in_specs=(
            P("tile", None, None),
            P("row", "tile", None, None),
            P("row", "tile"),
            P("row", "tile"),
            P("row", "tile"),
            P(),
        ),
        out_specs=P("tile", "row", None),
        check_vma=False,
    )
```

```python
import functools

import jax
import jax.numpy as jnp
from jax import lax
from jax.experimental import pallas as pl
from jax.experimental.pallas import tpu as pltpu
from jax.sharding import PartitionSpec as P

TS = 16
ATS = 8
SLAB = 96


def padded(x, sides, width):
    for axis, dim in sides:
        size, length = (lax.axis_size(axis), x.shape[dim])
        up = [(i, (i + 1) % size) for i in range(size)]
        down = [(j, i) for i, j in up]
        last = lax.slice_in_dim(x, length - width, length, axis=dim)
        first = lax.slice_in_dim(x, 0, width, axis=dim)
        before = lax.ppermute(last, axis, up)
        after = lax.ppermute(first, axis, down)
        x = jnp.concatenate([before, x, after], axis=dim)
    return x


def find_mirror(pair_list):
    first_orb = pair_list[:, 0]
    second = pair_list[:, 1]
    matches = (first_orb[:, None] == second[None, :]) & (second[:, None] == first_orb[None, :])
    columns = jnp.arange(pair_list.shape[0], dtype=jnp.int32)
    return jnp.sum(jnp.where(matches, columns[None, :], 0), axis=1)


def to_grid(totals, a_tiles, b_tiles):
    pair_count = totals.shape[1]
    shaped = totals.reshape(a_tiles, b_tiles, pair_count, ATS, TS)
    return jnp.transpose(shaped, (2, 0, 3, 1, 4)).reshape(pair_count, a_tiles * ATS, b_tiles * TS)


def shards(amplitudes, integrals, slot_ab, slot_cd, live_count, pair_list):
    highest = lax.Precision.HIGHEST
    tile_size = lax.axis_size("tile")
    row_size = lax.axis_size("row")
    tile_index = lax.axis_index("tile")
    shard_tiles = amplitudes.shape[0]
    pair_count = amplitudes.shape[1]
    extended = padded(amplitudes, (("tile", 0),), shard_tiles)
    blocks_all = integrals[0]
    ab_local = slot_ab[0]
    cd_global = slot_cd[0]
    owner_tile = cd_global // shard_tiles
    offset = (owner_tile - tile_index + 1 + tile_size) % tile_size
    ext_index = offset * shard_tiles + cd_global % shard_tiles
    live_total = live_count[0, 0]
    a_tiles = SLAB // (row_size * ATS)
    b_tiles = SLAB // TS
    tiles_ab = a_tiles * b_tiles
    block_width = integrals.shape[2]
    group_size = 8

    def block_step(block_index, totals):
        first_slot = block_index * group_size
        picked = lax.dynamic_slice_in_dim(ext_index, first_slot, group_size)
        ab_tiles = lax.dynamic_slice_in_dim(ab_local, first_slot, group_size)
        blocks = lax.dynamic_slice_in_dim(blocks_all, first_slot, group_size, 0)
        live_mask = (first_slot + jnp.arange(group_size, dtype=jnp.int32) < live_total).astype(
            jnp.float32
        )
        amp_tiles = jnp.take(extended, picked, axis=0)
        products = jnp.einsum(
            "spw,sbw->spb", amp_tiles, blocks, precision=highest, preferred_element_type=jnp.float32
        )
        one_hot = (ab_tiles[:, None] == jnp.arange(tiles_ab, dtype=jnp.int32)[None, :]).astype(
            jnp.float32
        ) * live_mask[:, None]
        return totals + jnp.einsum(
            "se,spb->epb", one_hot, products, precision=highest, preferred_element_type=jnp.float32
        )

    turn_count = (live_total + group_size - 1) // group_size
    start_totals = jnp.zeros((tiles_ab, pair_count, block_width), jnp.float32)
    totals = lax.fori_loop(0, turn_count, block_step, start_totals)
    whole_term = to_grid(totals, a_tiles, b_tiles)
    mirror = find_mirror(pair_list)
    reduced = lax.psum_scatter(whole_term, "tile", scatter_dimension=0, tiled=True)
    exchanged = lax.all_to_all(reduced, "row", split_axis=2, concat_axis=1, tiled=True)
    turned = jnp.transpose(exchanged, (0, 2, 1))
    everyone = lax.all_gather(turned, "tile", axis=0, tiled=True)
    local_pairs = reduced.shape[0]
    wanted = lax.dynamic_slice_in_dim(mirror, tile_index * local_pairs, local_pairs)
    return reduced + jnp.take(everyone, wanted, axis=0)


MESH = pl.DeviceIdType.MESH
CHUNK = 2
WINDOW = 4
GROUP = 8
AHEAD = 2
VMEM_BYTES = 56 * 1024 * 1024


def place():
    k = lax.axis_index("tile")
    r = lax.axis_index("row")
    return k, r, k // 2, k % 2


def greet(devices):
    barrier = pltpu.get_barrier_semaphore()
    for device in devices:
        pl.semaphore_signal(barrier, inc=1, device_id=device, device_id_type=MESH)
    pl.semaphore_wait(barrier, len(devices))


def halo_kernel(tiles, amp, halo, send, rx, rz, ry, rc):
    k, r, z, x = place()
    y, core = r // 2, r % 2
    sixth = tiles // 6
    half = sixth // CHUNK
    count = 2 * half
    other_x = (z * 2 + 1 - x, r)
    up = ((z + 1) % 4 * 2 + x, r)
    down = ((z + 3) % 4 * 2 + x, r)
    next_z = (jnp.where(x == 0, up[0], down[0]), r)
    other_y = (k, (1 - y) * 2 + core)
    other_core = (k, y * 2 + 1 - core)
    greet((other_x, up, down, other_y, other_core))

    def first_of(yy, cc, j):
        own = (yy * 2 + cc) * sixth + j * CHUNK
        both = (4 + cc) * sixth + (j - half) * CHUNK
        return own if j < half else both

    def remote(src, dst, sent, received, device):
        return pltpu.make_async_remote_copy(
            src_ref=src, dst_ref=dst, send_sem=sent, recv_sem=received, device_id=device, device_id_type=MESH
        )

    def at(side, first):
        return halo.at[pl.ds(side * tiles + first, CHUNK)]

    def copy_x(j):
        first = first_of(y, core, j)
        return remote(amp.at[pl.ds(first, CHUNK)], at(0, first), send.at[0, j], rx.at[j], other_x)

    def copy_z(j):
        first = first_of(y, core, j)
        return remote(at(0, first), at(1, first), send.at[1, j], rz.at[j], next_z)

    def copy_y(side, j):
        first = first_of(y, core, j)
        return remote(at(side, first), at(side, first), send.at[2 + side, j], ry.at[side, j], other_y)

    def copy_c(side, j):
        first = first_of(y, core, j) if j < count else first_of(1 - y, core, j - count)
        return remote(at(side, first), at(side, first), send.at[4 + side, j], rc.at[side, j], other_core)

    sends = []

    def go(copy):
        copy.start()
        sends.append(copy)

    for j in range(WINDOW):
        go(copy_x(j))
    lag = 1
    for i in range(count + 3 * lag):
        if i < count:
            copy_x(i).wait_recv()
            if i + WINDOW < count:
                go(copy_x(i + WINDOW))
            go(copy_z(i))
            if i < half:
                go(copy_y(0, i))
            go(copy_c(0, i))
        j = i - lag
        if 0 <= j < count:
            copy_z(j).wait_recv()
            if j < half:
                go(copy_y(1, j))
            go(copy_c(1, j))
        j = i - 2 * lag
        if 0 <= j < half:
            copy_y(0, j).wait_recv()
            go(copy_c(0, count + j))
        j = i - 3 * lag
        if 0 <= j < half:
            copy_y(1, j).wait_recv()
            go(copy_c(1, count + j))
    for j in range(count + half):
        for side in range(2):
            copy_c(side, j).wait_recv()
    for copy in sends:
        copy.wait_send()


def halo_of(amplitudes):
    tiles = amplitudes.shape[0]
    count = tiles // 3 // CHUNK
    return pl.pallas_call(
        functools.partial(halo_kernel, tiles),
        out_shape=jax.ShapeDtypeStruct((2 * tiles,) + amplitudes.shape[1:], jnp.float32),
        in_specs=[pl.BlockSpec(memory_space=pl.ANY)],
        out_specs=pl.BlockSpec(memory_space=pl.ANY),
        scratch_shapes=[
            pltpu.SemaphoreType.DMA((6, count + count // 2)),
            pltpu.SemaphoreType.DMA((count,)),
            pltpu.SemaphoreType.DMA((count,)),
            pltpu.SemaphoreType.DMA((2, count // 2)),
            pltpu.SemaphoreType.DMA((2, count + count // 2)),
        ],
        compiler_params=pltpu.CompilerParams(
            collective_id=0, has_side_effects=True, vmem_limit_bytes=VMEM_BYTES
        ),
    )(amplitudes)


def split(v):
    high = v.astype(jnp.bfloat16)
    low = (v - high.astype(jnp.float32)).astype(jnp.bfloat16)
    return jnp.concatenate([high, low], axis=0)


def slots_kernel(amp, halo, blocks, ab, cd, live, pairs, out, abuf, bbuf, asem, bsem, table):
    k = lax.axis_index("tile")
    tiles = amp.shape[0]
    pair_count = halo.shape[1]
    width = blocks.shape[1]
    groups = (live[0, 0] + GROUP - 1) // GROUP
    x = k % 2
    other_x = k + 1 - 2 * x
    next_z = lax.rem(k + 7 + 2 * x, 8)

    def block_copy(g):
        return pltpu.make_async_copy(
            blocks.at[pl.ds(g * GROUP, GROUP)], bbuf.at[pl.ds(g * GROUP, GROUP)], bsem.at[g]
        )

    def fetch(g):
        for i in range(GROUP):
            s = g * GROUP + i
            c = cd[0, s]
            mine = (c >= k * tiles) & (c < (k + 1) * tiles)
            beside = (c >= other_x * tiles) & (c < (other_x + 1) * tiles)
            shift = jnp.where(beside, -other_x, 1 - next_z)

            @pl.when(mine)
            def _():
                pltpu.make_async_copy(amp.at[c - k * tiles], abuf.at[s], asem.at[g]).start()

            @pl.when(jnp.logical_not(mine))
            def _():
                pltpu.make_async_copy(halo.at[c + shift * tiles], abuf.at[s], asem.at[g]).start()


    def start_blocks(g, carry):
        block_copy(g).start()
        return carry

    block_copy(0).start()
    fetch(0)
    lax.fori_loop(1, groups, start_blocks, 0)
    for g in range(1, AHEAD):
        pl.when(g < groups)(functools.partial(fetch, g))
    out[...] = jnp.zeros_like(out)

    def note(p, carry):
        table[pairs[p, 0] * 128 + pairs[p, 1]] = p
        return carry

    lax.fori_loop(0, pair_count, note, 0)

    def step(g, carry):
        base = g * GROUP
        pl.when(g + AHEAD < groups)(lambda: fetch(g + AHEAD))
        pltpu.make_async_copy(
            halo.at[pl.ds(0, GROUP)], abuf.at[pl.ds(base, GROUP)], asem.at[g]
        ).wait()
        block_copy(g).wait()
        terms = []
        for i in range(GROUP):
            left = split(abuf[base + i])
            right = split(bbuf[base + i])
            full = lax.dot_general(
                left, right, (((1,), (1,)), ((), ())), preferred_element_type=jnp.float32
            )
            top, low = full[:pair_count], full[pair_count:]
            terms.append(top[:, :width] + (top[:, width:] + (low[:, :width] + low[:, width:])))
        for i in range(GROUP):
            s = g * GROUP + i
            term = jnp.where(s < live[0, 0], terms[i], 0.0).reshape(out.shape[0], out.shape[3], width)
            e = ab[0, s]
            out[:, 0, e] += term
        return carry

    lax.fori_loop(0, groups, step, 0)

    def turn(p, carry):
        m = table[pairs[p, 1] * 128 + pairs[p, 0]]
        out[p // 8, 1, :, pl.ds(p % 8, 1), :] = out[m // 8, 0, :, pl.ds(m % 8, 1), :]
        return carry

    lax.fori_loop(0, pair_count, turn, 0)


def slot_sums(amplitudes, halo, blocks, ab, cd, live, pair_list, tiles_ab):
    pair_count, depth = halo.shape[1:]
    slots, width = blocks.shape[:2]
    anywhere = pl.BlockSpec(memory_space=pl.ANY)
    scalars = pl.BlockSpec(memory_space=pltpu.SMEM)
    return pl.pallas_call(
        slots_kernel,
        out_shape=jax.ShapeDtypeStruct((pair_count // 8, 2, tiles_ab, 8, width), jnp.float32),
        in_specs=[anywhere] * 3 + [scalars] * 4,
        out_specs=pl.BlockSpec(memory_space=pltpu.VMEM),
        scratch_shapes=[
            pltpu.VMEM((slots, pair_count, depth), jnp.float32),
            pltpu.VMEM((slots, width, depth), jnp.float32),
            pltpu.SemaphoreType.DMA((slots // GROUP,)),
            pltpu.SemaphoreType.DMA((slots // GROUP,)),
            pltpu.SMEM((128 * 128,), jnp.int32),
        ],
        compiler_params=pltpu.CompilerParams(vmem_limit_bytes=VMEM_BYTES),
    )(amplitudes, halo, blocks, ab, cd, live, pair_list)


def sum_kernel(sums, ladder, turned, bx, sz, bz, mine, send_x, recv_x, send_z, recv_z, send_r, recv_r):
    k, r, z, x = place()
    other_x = (z * 2 + 1 - x, r)
    zs = [((z + i) % 4 * 2 + x, r) for i in range(1, 4)]
    rows = [(k, (r + i) % 4) for i in range(1, 4)]
    greet([other_x] + zs + rows)

    def remote(src, dst, sent, received, device):
        return pltpu.make_async_remote_copy(
            src_ref=src, dst_ref=dst, send_sem=sent, recv_sem=received, device_id=device, device_id_type=MESH
        )

    steps = [(i, h) for i in (2, 1, 3, 0) for h in range(2)]
    over_x = {
        (i, h): remote(
            sums.at[(z + i) % 4 * 2 + 1 - x, h], bx.at[i, h], send_x.at[i, h], recv_x.at[i, h], other_x
        )
        for i, h in steps
    }
    over_z = {
        (i, h): remote(sz.at[i, h], bz.at[i, h], send_z.at[i, h], recv_z.at[i, h], zs[i - 1])
        for i, h in steps if i > 0
    }
    for step in steps[:WINDOW]:
        over_x[step].start()
    for j, (i, h) in enumerate(steps):
        over_x[i, h].wait_recv()
        if j + WINDOW < len(steps):
            over_x[steps[j + WINDOW]].start()
        total = bx[i, h] + sums[(z + i) % 4 * 2 + x, h]
        if i > 0:
            sz[i, h] = total
            over_z[i, h].start()
        else:
            mine[h] = total
    for i in (1, 3, 2):
        for h in range(2):
            over_z[i, h].wait_recv()
    total = mine[...] + bz[1] + bz[2] + bz[3]
    ladder[...] = total[0].reshape(ladder.shape)
    mine[...] = total
    parts = mine.at[1]

    def over_row(i):
        first = (r + i) % 4 * 3 // 2
        return [
            remote(
                parts.at[pl.ds(t * 6 + first, 2)], turned.at[r, t], send_r.at[i, t], recv_r.at[i, t], rows[i - 1]
            )
            for t in range(3)
        ]

    copies = [c for i in range(1, 4) for c in over_row(i)]
    for c in copies:
        c.start()
    own = r * 3 // 2
    for t in range(3):
        turned[r, t] = mine[1, pl.ds(t * 6 + own, 2)]
    for i in range(1, 4):
        source = (r + 4 - i) % 4
        for t in range(3):
            remote(
                parts.at[pl.ds(0, 2)], turned.at[source, t], send_r.at[i, t], recv_r.at[i, t], rows[i - 1]
            ).wait_recv()
    for c in copies + list(over_x.values()) + list(over_z.values()):
        c.wait_send()


def sum_over_tile(sums):
    chunk = sums.shape[1:]
    vmem = pl.BlockSpec(memory_space=pltpu.VMEM)
    dma = pltpu.SemaphoreType.DMA
    return pl.pallas_call(
        sum_kernel,
        out_shape=(
            jax.ShapeDtypeStruct((3, 6) + chunk[2:], jnp.float32),
            jax.ShapeDtypeStruct((4, 3, 2) + chunk[2:], jnp.float32),
        ),
        in_specs=[vmem],
        out_specs=(vmem, vmem),
        scratch_shapes=[
            pltpu.VMEM((4,) + chunk, jnp.float32),
            pltpu.VMEM((4,) + chunk, jnp.float32),
            pltpu.VMEM((4,) + chunk, jnp.float32),
            pltpu.VMEM(chunk, jnp.float32),
            dma((4, 2)), dma((4, 2)), dma((4, 2)), dma((4, 2)), dma((4, 3)), dma((4, 3)),
        ],
        compiler_params=pltpu.CompilerParams(
            collective_id=1, has_side_effects=True, vmem_limit_bytes=16 * 1024 * 1024
        ),
    )(sums)


def shards_8x4(amplitudes, integrals, slot_ab, slot_cd, live_count, pair_list):
    halo = halo_of(amplitudes)
    sums = slot_sums(amplitudes, halo, integrals[0], slot_ab, slot_cd, live_count, pair_list, 18)
    ladder, turned = sum_over_tile(sums)
    local_pairs = ladder.shape[2]
    grid = jnp.transpose(ladder.reshape(3, 6, local_pairs, ATS, TS), (2, 0, 3, 1, 4)).reshape(local_pairs, 24, SLAB)
    other = turned.reshape(4, 3, 2, local_pairs, ATS, TS)
    other = jnp.transpose(other, (3, 2, 5, 0, 1, 4)).reshape(local_pairs, 2 * TS, SLAB)
    shift = lax.axis_index("row") % 2 * 8
    return grid + lax.dynamic_slice_in_dim(other, shift, 24, axis=1)


def solution(mesh):
    fast = mesh.shape["tile"] == 8 and mesh.shape["row"] == 4
    return jax.shard_map(
        shards_8x4 if fast else shards,
        mesh=mesh,
        in_specs=(
            P("tile", None, None),
            P("row", "tile", None, None),
            P("row", "tile"),
            P("row", "tile"),
            P("row", "tile"),
            P(),
        ),
        out_specs=P("tile", "row", None),
        check_vma=False,
    )
```

```python
import functools

import jax
import jax.numpy as jnp
from jax import lax
from jax.experimental import pallas as pl
from jax.experimental.pallas import tpu as pltpu
from jax.sharding import PartitionSpec as P

TS = 16
ATS = 8
SLAB = 96


def padded(x, sides, width):
    for axis, dim in sides:
        size, length = (lax.axis_size(axis), x.shape[dim])
        up = [(i, (i + 1) % size) for i in range(size)]
        down = [(j, i) for i, j in up]
        last = lax.slice_in_dim(x, length - width, length, axis=dim)
        first = lax.slice_in_dim(x, 0, width, axis=dim)
        before = lax.ppermute(last, axis, up)
        after = lax.ppermute(first, axis, down)
        x = jnp.concatenate([before, x, after], axis=dim)
    return x


def find_mirror(pair_list):
    first_orb = pair_list[:, 0]
    second = pair_list[:, 1]
    matches = (first_orb[:, None] == second[None, :]) & (second[:, None] == first_orb[None, :])
    columns = jnp.arange(pair_list.shape[0], dtype=jnp.int32)
    return jnp.sum(jnp.where(matches, columns[None, :], 0), axis=1)


def to_grid(totals, a_tiles, b_tiles):
    pair_count = totals.shape[1]
    shaped = totals.reshape(a_tiles, b_tiles, pair_count, ATS, TS)
    return jnp.transpose(shaped, (2, 0, 3, 1, 4)).reshape(pair_count, a_tiles * ATS, b_tiles * TS)


def shards(amplitudes, integrals, slot_ab, slot_cd, live_count, pair_list):
    highest = lax.Precision.HIGHEST
    tile_size = lax.axis_size("tile")
    row_size = lax.axis_size("row")
    tile_index = lax.axis_index("tile")
    shard_tiles = amplitudes.shape[0]
    pair_count = amplitudes.shape[1]
    extended = padded(amplitudes, (("tile", 0),), shard_tiles)
    blocks_all = integrals[0]
    ab_local = slot_ab[0]
    cd_global = slot_cd[0]
    owner_tile = cd_global // shard_tiles
    offset = (owner_tile - tile_index + 1 + tile_size) % tile_size
    ext_index = offset * shard_tiles + cd_global % shard_tiles
    live_total = live_count[0, 0]
    a_tiles = SLAB // (row_size * ATS)
    b_tiles = SLAB // TS
    tiles_ab = a_tiles * b_tiles
    block_width = integrals.shape[2]
    group_size = 8

    def block_step(block_index, totals):
        first_slot = block_index * group_size
        picked = lax.dynamic_slice_in_dim(ext_index, first_slot, group_size)
        ab_tiles = lax.dynamic_slice_in_dim(ab_local, first_slot, group_size)
        blocks = lax.dynamic_slice_in_dim(blocks_all, first_slot, group_size, 0)
        live_mask = (first_slot + jnp.arange(group_size, dtype=jnp.int32) < live_total).astype(
            jnp.float32
        )
        amp_tiles = jnp.take(extended, picked, axis=0)
        products = jnp.einsum(
            "spw,sbw->spb", amp_tiles, blocks, precision=highest, preferred_element_type=jnp.float32
        )
        one_hot = (ab_tiles[:, None] == jnp.arange(tiles_ab, dtype=jnp.int32)[None, :]).astype(
            jnp.float32
        ) * live_mask[:, None]
        return totals + jnp.einsum(
            "se,spb->epb", one_hot, products, precision=highest, preferred_element_type=jnp.float32
        )

    turn_count = (live_total + group_size - 1) // group_size
    start_totals = jnp.zeros((tiles_ab, pair_count, block_width), jnp.float32)
    totals = lax.fori_loop(0, turn_count, block_step, start_totals)
    whole_term = to_grid(totals, a_tiles, b_tiles)
    mirror = find_mirror(pair_list)
    reduced = lax.psum_scatter(whole_term, "tile", scatter_dimension=0, tiled=True)
    exchanged = lax.all_to_all(reduced, "row", split_axis=2, concat_axis=1, tiled=True)
    turned = jnp.transpose(exchanged, (0, 2, 1))
    everyone = lax.all_gather(turned, "tile", axis=0, tiled=True)
    local_pairs = reduced.shape[0]
    wanted = lax.dynamic_slice_in_dim(mirror, tile_index * local_pairs, local_pairs)
    return reduced + jnp.take(everyone, wanted, axis=0)


MESH = pl.DeviceIdType.MESH
CHUNK = 2
WINDOW = 4
GROUP = 8
AHEAD = 2
VMEM_BYTES = 56 * 1024 * 1024


def place():
    k = lax.axis_index("tile")
    r = lax.axis_index("row")
    return k, r, k // 2, k % 2


def greet(devices):
    barrier = pltpu.get_barrier_semaphore()
    for device in devices:
        pl.semaphore_signal(barrier, inc=1, device_id=device, device_id_type=MESH)
    pl.semaphore_wait(barrier, len(devices))


def halo_kernel(tiles, amp, halo, send, rx, rz, ry, rc):
    k, r, z, x = place()
    y, core = r // 2, r % 2
    sixth = tiles // 6
    half = sixth // CHUNK
    count = 2 * half
    other_x = (z * 2 + 1 - x, r)
    up = ((z + 1) % 4 * 2 + x, r)
    down = ((z + 3) % 4 * 2 + x, r)
    next_z = (jnp.where(x == 0, up[0], down[0]), r)
    other_y = (k, (1 - y) * 2 + core)
    other_core = (k, y * 2 + 1 - core)
    greet((other_x, up, down, other_y, other_core))

    def first_of(yy, cc, j):
        own = (yy * 2 + cc) * sixth + j * CHUNK
        both = (4 + cc) * sixth + (j - half) * CHUNK
        return own if j < half else both

    def remote(src, dst, sent, received, device):
        return pltpu.make_async_remote_copy(
            src_ref=src, dst_ref=dst, send_sem=sent, recv_sem=received, device_id=device, device_id_type=MESH
        )

    def at(side, first):
        return halo.at[pl.ds(side * tiles + first, CHUNK)]

    def copy_x(j):
        first = first_of(y, core, j)
        return remote(amp.at[pl.ds(first, CHUNK)], at(0, first), send.at[0, j], rx.at[j], other_x)

    def copy_z(j):
        first = first_of(y, core, j)
        return remote(at(0, first), at(1, first), send.at[1, j], rz.at[j], next_z)

    def copy_y(side, j):
        first = first_of(y, core, j)
        return remote(at(side, first), at(side, first), send.at[2 + side, j], ry.at[side, j], other_y)

    def copy_c(side, j):
        first = first_of(y, core, j) if j < count else first_of(1 - y, core, j - count)
        return remote(at(side, first), at(side, first), send.at[4 + side, j], rc.at[side, j], other_core)

    sends = []

    def go(copy):
        copy.start()
        sends.append(copy)

    for j in range(WINDOW):
        go(copy_x(j))
    lag = 1
    for i in range(count + 3 * lag):
        if i < count:
            copy_x(i).wait_recv()
            if i + WINDOW < count:
                go(copy_x(i + WINDOW))
            go(copy_z(i))
            if i < half:
                go(copy_y(0, i))
            go(copy_c(0, i))
        j = i - lag
        if 0 <= j < count:
            copy_z(j).wait_recv()
            if j < half:
                go(copy_y(1, j))
            go(copy_c(1, j))
        j = i - 2 * lag
        if 0 <= j < half:
            copy_y(0, j).wait_recv()
            go(copy_c(0, count + j))
        j = i - 3 * lag
        if 0 <= j < half:
            copy_y(1, j).wait_recv()
            go(copy_c(1, count + j))
    for j in range(count + half):
        for side in range(2):
            copy_c(side, j).wait_recv()
    for copy in sends:
        copy.wait_send()


def halo_of(amplitudes):
    tiles = amplitudes.shape[0]
    count = tiles // 3 // CHUNK
    return pl.pallas_call(
        functools.partial(halo_kernel, tiles),
        out_shape=jax.ShapeDtypeStruct((2 * tiles,) + amplitudes.shape[1:], jnp.float32),
        in_specs=[pl.BlockSpec(memory_space=pl.ANY)],
        out_specs=pl.BlockSpec(memory_space=pltpu.VMEM),
        scratch_shapes=[
            pltpu.SemaphoreType.DMA((6, count + count // 2)),
            pltpu.SemaphoreType.DMA((count,)),
            pltpu.SemaphoreType.DMA((count,)),
            pltpu.SemaphoreType.DMA((2, count // 2)),
            pltpu.SemaphoreType.DMA((2, count + count // 2)),
        ],
        compiler_params=pltpu.CompilerParams(
            collective_id=0, has_side_effects=True, vmem_limit_bytes=VMEM_BYTES
        ),
    )(amplitudes)


def split(v):
    high = v.astype(jnp.bfloat16)
    low = (v - high.astype(jnp.float32)).astype(jnp.bfloat16)
    return jnp.concatenate([high, low], axis=0)


def slots_kernel(amp, halo, blocks, ab, cd, live, pairs, out, abuf, bbuf, asem, bsem, table):
    k = lax.axis_index("tile")
    tiles = amp.shape[0]
    pair_count = halo.shape[1]
    width = blocks.shape[1]
    groups = (live[0, 0] + GROUP - 1) // GROUP
    x = k % 2
    other_x = k + 1 - 2 * x
    next_z = lax.rem(k + 7 + 2 * x, 8)

    def block_copy(g):
        return pltpu.make_async_copy(
            blocks.at[pl.ds(g * GROUP, GROUP)], bbuf.at[pl.ds(g * GROUP, GROUP)], bsem.at[g]
        )

    def fetch(g):
        for i in range(GROUP):
            s = g * GROUP + i
            c = cd[0, s]
            mine = (c >= k * tiles) & (c < (k + 1) * tiles)
            beside = (c >= other_x * tiles) & (c < (other_x + 1) * tiles)
            shift = jnp.where(beside, -other_x, 1 - next_z)

            @pl.when(mine)
            def _():
                pltpu.make_async_copy(amp.at[c - k * tiles], abuf.at[s], asem.at[g]).start()

            @pl.when(jnp.logical_not(mine))
            def _():
                pltpu.make_async_copy(halo.at[c + shift * tiles], abuf.at[s], asem.at[g]).start()


    def start_blocks(g, carry):
        block_copy(g).start()
        return carry

    block_copy(0).start()
    fetch(0)
    lax.fori_loop(1, groups, start_blocks, 0)
    for g in range(1, AHEAD):
        pl.when(g < groups)(functools.partial(fetch, g))
    out[...] = jnp.zeros_like(out)

    def note(p, carry):
        table[pairs[p, 0] * 128 + pairs[p, 1]] = p
        return carry

    lax.fori_loop(0, pair_count, note, 0)

    def step(g, carry):
        base = g * GROUP
        pl.when(g + AHEAD < groups)(lambda: fetch(g + AHEAD))
        pltpu.make_async_copy(
            halo.at[pl.ds(0, GROUP)], abuf.at[pl.ds(base, GROUP)], asem.at[g]
        ).wait()
        block_copy(g).wait()
        terms = []
        for i in range(GROUP):
            left = split(abuf[base + i])
            right = split(bbuf[base + i])
            full = lax.dot_general(
                left, right, (((1,), (1,)), ((), ())), preferred_element_type=jnp.float32
            )
            top, low = full[:pair_count], full[pair_count:]
            terms.append(top[:, :width] + (top[:, width:] + (low[:, :width] + low[:, width:])))
        for i in range(GROUP):
            s = g * GROUP + i
            term = jnp.where(s < live[0, 0], terms[i], 0.0).reshape(out.shape[0], out.shape[3], width)
            e = ab[0, s]
            out[:, 0, e] += term
        return carry

    lax.fori_loop(0, groups, step, 0)

    def turn(p, carry):
        m = table[pairs[p, 1] * 128 + pairs[p, 0]]
        out[p // 8, 1, :, pl.ds(p % 8, 1), :] = out[m // 8, 0, :, pl.ds(m % 8, 1), :]
        return carry

    lax.fori_loop(0, pair_count, turn, 0)


def slot_sums(amplitudes, halo, blocks, ab, cd, live, pair_list, tiles_ab):
    pair_count, depth = halo.shape[1:]
    slots, width = blocks.shape[:2]
    anywhere = pl.BlockSpec(memory_space=pl.ANY)
    scalars = pl.BlockSpec(memory_space=pltpu.SMEM)
    return pl.pallas_call(
        slots_kernel,
        out_shape=jax.ShapeDtypeStruct((pair_count // 8, 2, tiles_ab, 8, width), jnp.float32),
        in_specs=[anywhere] * 3 + [scalars] * 4,
        out_specs=pl.BlockSpec(memory_space=pltpu.VMEM),
        scratch_shapes=[
            pltpu.VMEM((slots, pair_count, depth), jnp.float32),
            pltpu.VMEM((slots, width, depth), jnp.float32),
            pltpu.SemaphoreType.DMA((slots // GROUP,)),
            pltpu.SemaphoreType.DMA((slots // GROUP,)),
            pltpu.SMEM((128 * 128,), jnp.int32),
        ],
        compiler_params=pltpu.CompilerParams(vmem_limit_bytes=VMEM_BYTES),
    )(amplitudes, halo, blocks, ab, cd, live, pair_list)


def sum_kernel(sums, ladder, turned, bx, sz, bz, mine, send_x, recv_x, send_z, recv_z, send_r, recv_r):
    k, r, z, x = place()
    other_x = (z * 2 + 1 - x, r)
    zs = [((z + i) % 4 * 2 + x, r) for i in range(1, 4)]
    rows = [(k, (r + i) % 4) for i in range(1, 4)]
    greet([other_x] + zs + rows)

    def remote(src, dst, sent, received, device):
        return pltpu.make_async_remote_copy(
            src_ref=src, dst_ref=dst, send_sem=sent, recv_sem=received, device_id=device, device_id_type=MESH
        )

    steps = [(i, h) for i in (2, 1, 3, 0) for h in range(2)]
    over_x = {
        (i, h): remote(
            sums.at[(z + i) % 4 * 2 + 1 - x, h], bx.at[i, h], send_x.at[i, h], recv_x.at[i, h], other_x
        )
        for i, h in steps
    }
    over_z = {
        (i, h): remote(sz.at[i, h], bz.at[i, h], send_z.at[i, h], recv_z.at[i, h], zs[i - 1])
        for i, h in steps if i > 0
    }
    for step in steps[:WINDOW]:
        over_x[step].start()
    for j, (i, h) in enumerate(steps):
        over_x[i, h].wait_recv()
        if j + WINDOW < len(steps):
            over_x[steps[j + WINDOW]].start()
        total = bx[i, h] + sums[(z + i) % 4 * 2 + x, h]
        if i > 0:
            sz[i, h] = total
            over_z[i, h].start()
        else:
            mine[h] = total
    for i in (1, 3, 2):
        for h in range(2):
            over_z[i, h].wait_recv()
    total = mine[...] + bz[1] + bz[2] + bz[3]
    ladder[...] = total[0].reshape(ladder.shape)
    mine[...] = total
    parts = mine.at[1]

    def over_row(i):
        first = (r + i) % 4 * 3 // 2
        return [
            remote(
                parts.at[pl.ds(t * 6 + first, 2)], turned.at[r, t], send_r.at[i, t], recv_r.at[i, t], rows[i - 1]
            )
            for t in range(3)
        ]

    copies = [c for i in range(1, 4) for c in over_row(i)]
    for c in copies:
        c.start()
    own = r * 3 // 2
    for t in range(3):
        turned[r, t] = mine[1, pl.ds(t * 6 + own, 2)]
    for i in range(1, 4):
        source = (r + 4 - i) % 4
        for t in range(3):
            remote(
                parts.at[pl.ds(0, 2)], turned.at[source, t], send_r.at[i, t], recv_r.at[i, t], rows[i - 1]
            ).wait_recv()
    for c in copies + list(over_x.values()) + list(over_z.values()):
        c.wait_send()


def sum_over_tile(sums):
    chunk = sums.shape[1:]
    vmem = pl.BlockSpec(memory_space=pltpu.VMEM)
    dma = pltpu.SemaphoreType.DMA
    return pl.pallas_call(
        sum_kernel,
        out_shape=(
            jax.ShapeDtypeStruct((3, 6) + chunk[2:], jnp.float32),
            jax.ShapeDtypeStruct((4, 3, 2) + chunk[2:], jnp.float32),
        ),
        in_specs=[vmem],
        out_specs=(vmem, vmem),
        scratch_shapes=[
            pltpu.VMEM((4,) + chunk, jnp.float32),
            pltpu.VMEM((4,) + chunk, jnp.float32),
            pltpu.VMEM((4,) + chunk, jnp.float32),
            pltpu.VMEM(chunk, jnp.float32),
            dma((4, 2)), dma((4, 2)), dma((4, 2)), dma((4, 2)), dma((4, 3)), dma((4, 3)),
        ],
        compiler_params=pltpu.CompilerParams(
            collective_id=1, has_side_effects=True, vmem_limit_bytes=16 * 1024 * 1024
        ),
    )(sums)


def shards_8x4(amplitudes, integrals, slot_ab, slot_cd, live_count, pair_list):
    halo = halo_of(amplitudes)
    sums = slot_sums(amplitudes, halo, integrals[0], slot_ab, slot_cd, live_count, pair_list, 18)
    ladder, turned = sum_over_tile(sums)
    local_pairs = ladder.shape[2]
    grid = jnp.transpose(ladder.reshape(3, 6, local_pairs, ATS, TS), (2, 0, 3, 1, 4)).reshape(local_pairs, 24, SLAB)
    other = turned.reshape(4, 3, 2, local_pairs, ATS, TS)
    other = jnp.transpose(other, (3, 2, 5, 0, 1, 4)).reshape(local_pairs, 2 * TS, SLAB)
    shift = lax.axis_index("row") % 2 * 8
    return grid + lax.dynamic_slice_in_dim(other, shift, 24, axis=1)


def solution(mesh):
    fast = mesh.shape["tile"] == 8 and mesh.shape["row"] == 4
    return jax.shard_map(
        shards_8x4 if fast else shards,
        mesh=mesh,
        in_specs=(
            P("tile", None, None),
            P("row", "tile", None, None),
            P("row", "tile"),
            P("row", "tile"),
            P("row", "tile"),
            P(),
        ),
        out_specs=P("tile", "row", None),
        check_vma=False,
    )
```

```python
import functools

import jax
import jax.numpy as jnp
from jax import lax
from jax.experimental import pallas as pl
from jax.experimental.pallas import tpu as pltpu
from jax.sharding import PartitionSpec as P

TS = 16
ATS = 8
SLAB = 96


def padded(x, sides, width):
    for axis, dim in sides:
        size, length = (lax.axis_size(axis), x.shape[dim])
        up = [(i, (i + 1) % size) for i in range(size)]
        down = [(j, i) for i, j in up]
        last = lax.slice_in_dim(x, length - width, length, axis=dim)
        first = lax.slice_in_dim(x, 0, width, axis=dim)
        before = lax.ppermute(last, axis, up)
        after = lax.ppermute(first, axis, down)
        x = jnp.concatenate([before, x, after], axis=dim)
    return x


def find_mirror(pair_list):
    first_orb = pair_list[:, 0]
    second = pair_list[:, 1]
    matches = (first_orb[:, None] == second[None, :]) & (second[:, None] == first_orb[None, :])
    columns = jnp.arange(pair_list.shape[0], dtype=jnp.int32)
    return jnp.sum(jnp.where(matches, columns[None, :], 0), axis=1)


def to_grid(totals, a_tiles, b_tiles):
    pair_count = totals.shape[1]
    shaped = totals.reshape(a_tiles, b_tiles, pair_count, ATS, TS)
    return jnp.transpose(shaped, (2, 0, 3, 1, 4)).reshape(pair_count, a_tiles * ATS, b_tiles * TS)


def shards(amplitudes, integrals, slot_ab, slot_cd, live_count, pair_list):
    highest = lax.Precision.HIGHEST
    tile_size = lax.axis_size("tile")
    row_size = lax.axis_size("row")
    tile_index = lax.axis_index("tile")
    shard_tiles = amplitudes.shape[0]
    pair_count = amplitudes.shape[1]
    extended = padded(amplitudes, (("tile", 0),), shard_tiles)
    blocks_all = integrals[0]
    ab_local = slot_ab[0]
    cd_global = slot_cd[0]
    owner_tile = cd_global // shard_tiles
    offset = (owner_tile - tile_index + 1 + tile_size) % tile_size
    ext_index = offset * shard_tiles + cd_global % shard_tiles
    live_total = live_count[0, 0]
    a_tiles = SLAB // (row_size * ATS)
    b_tiles = SLAB // TS
    tiles_ab = a_tiles * b_tiles
    block_width = integrals.shape[2]
    group_size = 8

    def block_step(block_index, totals):
        first_slot = block_index * group_size
        picked = lax.dynamic_slice_in_dim(ext_index, first_slot, group_size)
        ab_tiles = lax.dynamic_slice_in_dim(ab_local, first_slot, group_size)
        blocks = lax.dynamic_slice_in_dim(blocks_all, first_slot, group_size, 0)
        live_mask = (first_slot + jnp.arange(group_size, dtype=jnp.int32) < live_total).astype(
            jnp.float32
        )
        amp_tiles = jnp.take(extended, picked, axis=0)
        products = jnp.einsum(
            "spw,sbw->spb", amp_tiles, blocks, precision=highest, preferred_element_type=jnp.float32
        )
        one_hot = (ab_tiles[:, None] == jnp.arange(tiles_ab, dtype=jnp.int32)[None, :]).astype(
            jnp.float32
        ) * live_mask[:, None]
        return totals + jnp.einsum(
            "se,spb->epb", one_hot, products, precision=highest, preferred_element_type=jnp.float32
        )

    turn_count = (live_total + group_size - 1) // group_size
    start_totals = jnp.zeros((tiles_ab, pair_count, block_width), jnp.float32)
    totals = lax.fori_loop(0, turn_count, block_step, start_totals)
    whole_term = to_grid(totals, a_tiles, b_tiles)
    mirror = find_mirror(pair_list)
    reduced = lax.psum_scatter(whole_term, "tile", scatter_dimension=0, tiled=True)
    exchanged = lax.all_to_all(reduced, "row", split_axis=2, concat_axis=1, tiled=True)
    turned = jnp.transpose(exchanged, (0, 2, 1))
    everyone = lax.all_gather(turned, "tile", axis=0, tiled=True)
    local_pairs = reduced.shape[0]
    wanted = lax.dynamic_slice_in_dim(mirror, tile_index * local_pairs, local_pairs)
    return reduced + jnp.take(everyone, wanted, axis=0)


MESH = pl.DeviceIdType.MESH
PIECES = 36
DIRECT = 14
ACROSS = 8
WINDOW = 4
LAG = 2
GROUP = 8
AHEAD = 2
VMEM_BYTES = 56 * 1024 * 1024


def place():
    k = lax.axis_index("tile")
    r = lax.axis_index("row")
    return k, r, k // 2, k % 2


def greet(devices):
    barrier = pltpu.get_barrier_semaphore()
    for device in devices:
        pl.semaphore_signal(barrier, inc=1, device_id=device, device_id_type=MESH)
    pl.semaphore_wait(barrier, len(devices))


def halo_kernel(tiles, amp, halo, send, rx, rz, ry, rc):
    k, r, z, x = place()
    y, core = r // 2, r % 2
    chunk = tiles // PIECES
    other_x = (z * 2 + 1 - x, r)
    up = ((z + 1) % 4 * 2 + x, r)
    down = ((z + 3) % 4 * 2 + x, r)
    next_z = (jnp.where(x == 0, up[0], down[0]), r)
    other_y = (k, (1 - y) * 2 + core)
    other_core = (k, y * 2 + 1 - core)
    greet((other_x, up, down, other_y, other_core))

    def first_of(cc, j):
        return (cc * (PIECES - 1) + (1 - 2 * cc) * j) * chunk

    def direct(i):
        return first_of(core, i + DIRECT * y if i < ACROSS else i)

    def remote(src, dst, sent, received, device):
        return pltpu.make_async_remote_copy(
            src_ref=src, dst_ref=dst, send_sem=sent, recv_sem=received, device_id=device, device_id_type=MESH
        )

    def at(side, first):
        return halo.at[pl.ds(side * tiles + first, chunk)]

    def copy_x(i):
        first = direct(i)
        return remote(amp.at[pl.ds(first, chunk)], at(0, first), send.at[0, i], rx.at[i], other_x)

    def copy_z(i):
        first = direct(i)
        return remote(at(0, first), at(1, first), send.at[1, i], rz.at[i], next_z)

    def copy_y(side, i):
        first = direct(i)
        return remote(at(side, first), at(side, first), send.at[2 + side, i], ry.at[side, i], other_y)

    def copy_c(side, i):
        first = first_of(core, i)
        return remote(at(side, first), at(side, first), send.at[4 + side, i], rc.at[side, i], other_core)

    sends = []

    def go(copy):
        copy.start()
        sends.append(copy)

    def hand_on(side, i):
        if i < ACROSS:
            go(copy_y(side, i))
            sends.append(copy_c(side, i))
            pl.when(y == 0)(lambda: copy_c(side, i).start())
        else:
            go(copy_c(side, i))

    def across(side, i):
        copy_y(side, i).wait_recv()
        pl.when(y == 1)(lambda: copy_c(side, i).start())

    for i in range(WINDOW):
        go(copy_x(i))
    for i in range(DIRECT + LAG):
        if i < DIRECT:
            copy_x(i).wait_recv()
            if i + WINDOW < DIRECT:
                go(copy_x(i + WINDOW))
            go(copy_z(i))
            hand_on(0, i)
        if i >= LAG:
            copy_z(i - LAG).wait_recv()
            hand_on(1, i - LAG)
        for side in range(2):
            if 0 <= i - LAG * (2 + side) < ACROSS:
                across(side, i - LAG * (2 + side))
    for side in range(2):
        for i in range(ACROSS):
            if i + LAG * (2 + side) >= DIRECT + LAG:
                across(side, i)
    for i in range(DIRECT):
        for side in range(2):
            copy_c(side, i).wait_recv()
    for copy in sends:
        copy.wait_send()


def halo_of(amplitudes):
    tiles = amplitudes.shape[0]
    return pl.pallas_call(
        functools.partial(halo_kernel, tiles),
        out_shape=jax.ShapeDtypeStruct((2 * tiles,) + amplitudes.shape[1:], jnp.float32),
        in_specs=[pl.BlockSpec(memory_space=pl.ANY)],
        out_specs=pl.BlockSpec(memory_space=pl.ANY),
        scratch_shapes=[
            pltpu.SemaphoreType.DMA((6, DIRECT)),
            pltpu.SemaphoreType.DMA((DIRECT,)),
            pltpu.SemaphoreType.DMA((DIRECT,)),
            pltpu.SemaphoreType.DMA((2, ACROSS)),
            pltpu.SemaphoreType.DMA((2, DIRECT)),
        ],
        compiler_params=pltpu.CompilerParams(
            collective_id=0, has_side_effects=True, vmem_limit_bytes=VMEM_BYTES
        ),
    )(amplitudes)


def split(v):
    high = v.astype(jnp.bfloat16)
    low = (v - high.astype(jnp.float32)).astype(jnp.bfloat16)
    return jnp.concatenate([high, low], axis=0)


def slots_kernel(amp, halo, blocks, ab, cd, live, pairs, out, abuf, bbuf, asem, bsem, table):
    k = lax.axis_index("tile")
    tiles = amp.shape[0]
    pair_count = halo.shape[1]
    width = blocks.shape[1]
    groups = (live[0, 0] + GROUP - 1) // GROUP
    x = k % 2
    other_x = k + 1 - 2 * x
    next_z = lax.rem(k + 7 + 2 * x, 8)

    def block_copy(g):
        return pltpu.make_async_copy(
            blocks.at[pl.ds(g * GROUP, GROUP)], bbuf.at[pl.ds(g * GROUP, GROUP)], bsem.at[g]
        )

    def fetch(g):
        for i in range(GROUP):
            s = g * GROUP + i
            c = cd[0, s]
            mine = (c >= k * tiles) & (c < (k + 1) * tiles)
            beside = (c >= other_x * tiles) & (c < (other_x + 1) * tiles)
            shift = jnp.where(beside, -other_x, 1 - next_z)

            @pl.when(mine)
            def _():
                pltpu.make_async_copy(amp.at[c - k * tiles], abuf.at[s], asem.at[g]).start()

            @pl.when(jnp.logical_not(mine))
            def _():
                pltpu.make_async_copy(halo.at[c + shift * tiles], abuf.at[s], asem.at[g]).start()


    def start_blocks(g, carry):
        block_copy(g).start()
        return carry

    block_copy(0).start()
    fetch(0)
    lax.fori_loop(1, groups, start_blocks, 0)
    for g in range(1, AHEAD):
        pl.when(g < groups)(functools.partial(fetch, g))
    out[...] = jnp.zeros_like(out)

    def note(p, carry):
        table[pairs[p, 0] * 128 + pairs[p, 1]] = p
        return carry

    lax.fori_loop(0, pair_count, note, 0)

    def step(g, carry):
        base = g * GROUP
        pl.when(g + AHEAD < groups)(lambda: fetch(g + AHEAD))
        pltpu.make_async_copy(
            halo.at[pl.ds(0, GROUP)], abuf.at[pl.ds(base, GROUP)], asem.at[g]
        ).wait()
        block_copy(g).wait()
        terms = []
        for i in range(GROUP):
            left = split(abuf[base + i])
            right = split(bbuf[base + i])
            full = lax.dot_general(
                left, right, (((1,), (1,)), ((), ())), preferred_element_type=jnp.float32
            )
            top, low = full[:pair_count], full[pair_count:]
            terms.append(top[:, :width] + (top[:, width:] + (low[:, :width] + low[:, width:])))
        for i in range(GROUP):
            s = g * GROUP + i
            term = jnp.where(s < live[0, 0], terms[i], 0.0).reshape(out.shape[0], out.shape[3], width)
            e = ab[0, s]
            out[:, 0, e] += term
        return carry

    lax.fori_loop(0, groups, step, 0)

    def turn(p, carry):
        m = table[pairs[p, 1] * 128 + pairs[p, 0]]
        out[p // 8, 1, :, pl.ds(p % 8, 1), :] = out[m // 8, 0, :, pl.ds(m % 8, 1), :]
        return carry

    lax.fori_loop(0, pair_count, turn, 0)


def slot_sums(amplitudes, halo, blocks, ab, cd, live, pair_list, tiles_ab):
    pair_count, depth = halo.shape[1:]
    slots, width = blocks.shape[:2]
    anywhere = pl.BlockSpec(memory_space=pl.ANY)
    scalars = pl.BlockSpec(memory_space=pltpu.SMEM)
    return pl.pallas_call(
        slots_kernel,
        out_shape=jax.ShapeDtypeStruct((pair_count // 8, 2, tiles_ab, 8, width), jnp.float32),
        in_specs=[anywhere] * 3 + [scalars] * 4,
        out_specs=pl.BlockSpec(memory_space=pltpu.VMEM),
        scratch_shapes=[
            pltpu.VMEM((slots, pair_count, depth), jnp.float32),
            pltpu.VMEM((slots, width, depth), jnp.float32),
            pltpu.SemaphoreType.DMA((slots // GROUP,)),
            pltpu.SemaphoreType.DMA((slots // GROUP,)),
            pltpu.SMEM((128 * 128,), jnp.int32),
        ],
        compiler_params=pltpu.CompilerParams(vmem_limit_bytes=VMEM_BYTES),
    )(amplitudes, halo, blocks, ab, cd, live, pair_list)


def sum_kernel(sums, ladder, turned, bx, sz, bz, mine, send_x, recv_x, send_z, recv_z, send_r, recv_r):
    k, r, z, x = place()
    other_x = (z * 2 + 1 - x, r)
    zs = [((z + i) % 4 * 2 + x, r) for i in range(1, 4)]
    rows = [(k, (r + i) % 4) for i in range(1, 4)]
    greet([other_x] + zs + rows)

    def remote(src, dst, sent, received, device):
        return pltpu.make_async_remote_copy(
            src_ref=src, dst_ref=dst, send_sem=sent, recv_sem=received, device_id=device, device_id_type=MESH
        )

    steps = [(i, h) for i in (2, 1, 3, 0) for h in range(2)]
    over_x = {
        (i, h): remote(
            sums.at[(z + i) % 4 * 2 + 1 - x, h], bx.at[i, h], send_x.at[i, h], recv_x.at[i, h], other_x
        )
        for i, h in steps
    }
    over_z = {
        (i, h): remote(sz.at[i, h], bz.at[i, h], send_z.at[i, h], recv_z.at[i, h], zs[i - 1])
        for i, h in steps if i > 0
    }
    for step in steps[:WINDOW]:
        over_x[step].start()
    for j, (i, h) in enumerate(steps):
        over_x[i, h].wait_recv()
        if j + WINDOW < len(steps):
            over_x[steps[j + WINDOW]].start()
        total = bx[i, h] + sums[(z + i) % 4 * 2 + x, h]
        if i > 0:
            sz[i, h] = total
            over_z[i, h].start()
        else:
            mine[h] = total
    for i in (1, 3, 2):
        for h in range(2):
            over_z[i, h].wait_recv()
    total = mine[...] + bz[1] + bz[2] + bz[3]
    ladder[...] = total[0].reshape(ladder.shape)
    mine[...] = total
    parts = mine.at[1]

    def over_row(i):
        first = (r + i) % 4 * 3 // 2
        return [
            remote(
                parts.at[pl.ds(t * 6 + first, 2)], turned.at[r, t], send_r.at[i, t], recv_r.at[i, t], rows[i - 1]
            )
            for t in range(3)
        ]

    copies = [c for i in range(1, 4) for c in over_row(i)]
    for c in copies:
        c.start()
    own = r * 3 // 2
    for t in range(3):
        turned[r, t] = mine[1, pl.ds(t * 6 + own, 2)]
    for i in range(1, 4):
        source = (r + 4 - i) % 4
        for t in range(3):
            remote(
                parts.at[pl.ds(0, 2)], turned.at[source, t], send_r.at[i, t], recv_r.at[i, t], rows[i - 1]
            ).wait_recv()
    for c in copies + list(over_x.values()) + list(over_z.values()):
        c.wait_send()


def sum_over_tile(sums):
    chunk = sums.shape[1:]
    vmem = pl.BlockSpec(memory_space=pltpu.VMEM)
    dma = pltpu.SemaphoreType.DMA
    return pl.pallas_call(
        sum_kernel,
        out_shape=(
            jax.ShapeDtypeStruct((3, 6) + chunk[2:], jnp.float32),
            jax.ShapeDtypeStruct((4, 3, 2) + chunk[2:], jnp.float32),
        ),
        in_specs=[vmem],
        out_specs=(vmem, vmem),
        scratch_shapes=[
            pltpu.VMEM((4,) + chunk, jnp.float32),
            pltpu.VMEM((4,) + chunk, jnp.float32),
            pltpu.VMEM((4,) + chunk, jnp.float32),
            pltpu.VMEM(chunk, jnp.float32),
            dma((4, 2)), dma((4, 2)), dma((4, 2)), dma((4, 2)), dma((4, 3)), dma((4, 3)),
        ],
        compiler_params=pltpu.CompilerParams(
            collective_id=1, has_side_effects=True, vmem_limit_bytes=16 * 1024 * 1024
        ),
    )(sums)


def shards_8x4(amplitudes, integrals, slot_ab, slot_cd, live_count, pair_list):
    halo = halo_of(amplitudes)
    sums = slot_sums(amplitudes, halo, integrals[0], slot_ab, slot_cd, live_count, pair_list, 18)
    ladder, turned = sum_over_tile(sums)
    local_pairs = ladder.shape[2]
    grid = jnp.transpose(ladder.reshape(3, 6, local_pairs, ATS, TS), (2, 0, 3, 1, 4)).reshape(local_pairs, 24, SLAB)
    other = turned.reshape(4, 3, 2, local_pairs, ATS, TS)
    other = jnp.transpose(other, (3, 2, 5, 0, 1, 4)).reshape(local_pairs, 2 * TS, SLAB)
    shift = lax.axis_index("row") % 2 * 8
    return grid + lax.dynamic_slice_in_dim(other, shift, 24, axis=1)


def solution(mesh):
    fast = mesh.shape["tile"] == 8 and mesh.shape["row"] == 4
    return jax.shard_map(
        shards_8x4 if fast else shards,
        mesh=mesh,
        in_specs=(
            P("tile", None, None),
            P("row", "tile", None, None),
            P("row", "tile"),
            P("row", "tile"),
            P("row", "tile"),
            P(),
        ),
        out_specs=P("tile", "row", None),
        check_vma=False,
    )
```

```python
import functools

import jax
import jax.numpy as jnp
from jax import lax
from jax.experimental import pallas as pl
from jax.experimental.pallas import tpu as pltpu
from jax.sharding import PartitionSpec as P

TS = 16
ATS = 8
SLAB = 96


def padded(x, sides, width):
    for axis, dim in sides:
        size, length = (lax.axis_size(axis), x.shape[dim])
        up = [(i, (i + 1) % size) for i in range(size)]
        down = [(j, i) for i, j in up]
        last = lax.slice_in_dim(x, length - width, length, axis=dim)
        first = lax.slice_in_dim(x, 0, width, axis=dim)
        before = lax.ppermute(last, axis, up)
        after = lax.ppermute(first, axis, down)
        x = jnp.concatenate([before, x, after], axis=dim)
    return x


def find_mirror(pair_list):
    first_orb = pair_list[:, 0]
    second = pair_list[:, 1]
    matches = (first_orb[:, None] == second[None, :]) & (second[:, None] == first_orb[None, :])
    columns = jnp.arange(pair_list.shape[0], dtype=jnp.int32)
    return jnp.sum(jnp.where(matches, columns[None, :], 0), axis=1)


def to_grid(totals, a_tiles, b_tiles):
    pair_count = totals.shape[1]
    shaped = totals.reshape(a_tiles, b_tiles, pair_count, ATS, TS)
    return jnp.transpose(shaped, (2, 0, 3, 1, 4)).reshape(pair_count, a_tiles * ATS, b_tiles * TS)


def shards(amplitudes, integrals, slot_ab, slot_cd, live_count, pair_list):
    highest = lax.Precision.HIGHEST
    tile_size = lax.axis_size("tile")
    row_size = lax.axis_size("row")
    tile_index = lax.axis_index("tile")
    shard_tiles = amplitudes.shape[0]
    pair_count = amplitudes.shape[1]
    extended = padded(amplitudes, (("tile", 0),), shard_tiles)
    blocks_all = integrals[0]
    ab_local = slot_ab[0]
    cd_global = slot_cd[0]
    owner_tile = cd_global // shard_tiles
    offset = (owner_tile - tile_index + 1 + tile_size) % tile_size
    ext_index = offset * shard_tiles + cd_global % shard_tiles
    live_total = live_count[0, 0]
    a_tiles = SLAB // (row_size * ATS)
    b_tiles = SLAB // TS
    tiles_ab = a_tiles * b_tiles
    block_width = integrals.shape[2]
    group_size = 8

    def block_step(block_index, totals):
        first_slot = block_index * group_size
        picked = lax.dynamic_slice_in_dim(ext_index, first_slot, group_size)
        ab_tiles = lax.dynamic_slice_in_dim(ab_local, first_slot, group_size)
        blocks = lax.dynamic_slice_in_dim(blocks_all, first_slot, group_size, 0)
        live_mask = (first_slot + jnp.arange(group_size, dtype=jnp.int32) < live_total).astype(
            jnp.float32
        )
        amp_tiles = jnp.take(extended, picked, axis=0)
        products = jnp.einsum(
            "spw,sbw->spb", amp_tiles, blocks, precision=highest, preferred_element_type=jnp.float32
        )
        one_hot = (ab_tiles[:, None] == jnp.arange(tiles_ab, dtype=jnp.int32)[None, :]).astype(
            jnp.float32
        ) * live_mask[:, None]
        return totals + jnp.einsum(
            "se,spb->epb", one_hot, products, precision=highest, preferred_element_type=jnp.float32
        )

    turn_count = (live_total + group_size - 1) // group_size
    start_totals = jnp.zeros((tiles_ab, pair_count, block_width), jnp.float32)
    totals = lax.fori_loop(0, turn_count, block_step, start_totals)
    whole_term = to_grid(totals, a_tiles, b_tiles)
    mirror = find_mirror(pair_list)
    reduced = lax.psum_scatter(whole_term, "tile", scatter_dimension=0, tiled=True)
    exchanged = lax.all_to_all(reduced, "row", split_axis=2, concat_axis=1, tiled=True)
    turned = jnp.transpose(exchanged, (0, 2, 1))
    everyone = lax.all_gather(turned, "tile", axis=0, tiled=True)
    local_pairs = reduced.shape[0]
    wanted = lax.dynamic_slice_in_dim(mirror, tile_index * local_pairs, local_pairs)
    return reduced + jnp.take(everyone, wanted, axis=0)


MESH = pl.DeviceIdType.MESH
CHUNK = 2
WINDOW = 4
GROUP = 8
AHEAD = 2


def place():
    k = lax.axis_index("tile")
    r = lax.axis_index("row")
    return k, r, k // 2, k % 2


def greet(devices):
    barrier = pltpu.get_barrier_semaphore()
    for device in devices:
        pl.semaphore_signal(barrier, inc=1, device_id=device, device_id_type=MESH)
    pl.semaphore_wait(barrier, len(devices))


def halo_kernel(tiles, amp, halo, send, rx, rz, ry, rc):
    k, r, z, x = place()
    y, core = r // 2, r % 2
    sixth = tiles // 6
    half = sixth // CHUNK
    count = 2 * half
    other_x = (z * 2 + 1 - x, r)
    up = ((z + 1) % 4 * 2 + x, r)
    down = ((z + 3) % 4 * 2 + x, r)
    next_z = (jnp.where(x == 0, up[0], down[0]), r)
    other_y = (k, (1 - y) * 2 + core)
    other_core = (k, y * 2 + 1 - core)
    greet((other_x, up, down, other_y, other_core))

    def first_of(yy, cc, j):
        own = (yy * 2 + cc) * sixth + j * CHUNK
        both = (4 + cc) * sixth + (j - half) * CHUNK
        return own if j < half else both

    def remote(src, dst, sent, received, device):
        return pltpu.make_async_remote_copy(
            src_ref=src, dst_ref=dst, send_sem=sent, recv_sem=received, device_id=device, device_id_type=MESH
        )

    def at(side, first):
        return halo.at[pl.ds(side * tiles + first, CHUNK)]

    def copy_x(j):
        first = first_of(y, core, j)
        return remote(amp.at[pl.ds(first, CHUNK)], at(0, first), send.at[0, j], rx.at[j], other_x)

    def copy_z(j):
        first = first_of(y, core, j)
        return remote(at(0, first), at(1, first), send.at[1, j], rz.at[j], next_z)

    def copy_y(side, j):
        first = first_of(y, core, j)
        return remote(at(side, first), at(side, first), send.at[2 + side, j], ry.at[side, j], other_y)

    def copy_c(side, j):
        first = first_of(y, core, j) if j < count else first_of(1 - y, core, j - count)
        return remote(at(side, first), at(side, first), send.at[4 + side, j], rc.at[side, j], other_core)

    sends = []

    def go(copy):
        copy.start()
        sends.append(copy)

    for j in range(WINDOW):
        go(copy_x(j))
    lag = 1
    for i in range(count + 3 * lag):
        if i < count:
            copy_x(i).wait_recv()
            if i + WINDOW < count:
                go(copy_x(i + WINDOW))
            go(copy_z(i))
            if i < half:
                go(copy_y(0, i))
            go(copy_c(0, i))
        j = i - lag
        if 0 <= j < count:
            copy_z(j).wait_recv()
            if j < half:
                go(copy_y(1, j))
            go(copy_c(1, j))
        j = i - 2 * lag
        if 0 <= j < half:
            copy_y(0, j).wait_recv()
            go(copy_c(0, count + j))
        j = i - 3 * lag
        if 0 <= j < half:
            copy_y(1, j).wait_recv()
            go(copy_c(1, count + j))
    for j in range(count + half):
        for side in range(2):
            copy_c(side, j).wait_recv()
    for copy in sends:
        copy.wait_send()


def halo_of(amplitudes):
    tiles = amplitudes.shape[0]
    count = tiles // 3 // CHUNK
    return pl.pallas_call(
        functools.partial(halo_kernel, tiles),
        out_shape=jax.ShapeDtypeStruct((2 * tiles,) + amplitudes.shape[1:], jnp.float32),
        in_specs=[pl.BlockSpec(memory_space=pl.ANY)],
        out_specs=pl.BlockSpec(memory_space=pl.ANY),
        scratch_shapes=[
            pltpu.SemaphoreType.DMA((6, count + count // 2)),
            pltpu.SemaphoreType.DMA((count,)),
            pltpu.SemaphoreType.DMA((count,)),
            pltpu.SemaphoreType.DMA((2, count // 2)),
            pltpu.SemaphoreType.DMA((2, count + count // 2)),
        ],
        compiler_params=pltpu.CompilerParams(
            collective_id=0, has_side_effects=True, vmem_limit_bytes=1024 * 1024
        ),
    )(amplitudes)


def split(v):
    high = v.astype(jnp.bfloat16)
    low = (v - high.astype(jnp.float32)).astype(jnp.bfloat16)
    return jnp.concatenate([high, low], axis=0)


def slots_kernel(amp, halo, blocks, ab, cd, live, pairs, out, abuf, bbuf, asem, bsem, table):
    k = lax.axis_index("tile")
    tiles = amp.shape[0]
    pair_count = halo.shape[1]
    width = blocks.shape[1]
    groups = (live[0, 0] + GROUP - 1) // GROUP
    x = k % 2
    other_x = k + 1 - 2 * x
    next_z = lax.rem(k + 7 + 2 * x, 8)

    def block_copy(g):
        return pltpu.make_async_copy(
            blocks.at[pl.ds(g * GROUP, GROUP)], bbuf.at[pl.ds(g * GROUP, GROUP)], bsem.at[g]
        )

    def fetch(g):
        for i in range(GROUP):
            s = g * GROUP + i
            c = cd[0, s]
            mine = (c >= k * tiles) & (c < (k + 1) * tiles)
            beside = (c >= other_x * tiles) & (c < (other_x + 1) * tiles)
            shift = jnp.where(beside, -other_x, 1 - next_z)

            @pl.when(mine)
            def _():
                pltpu.make_async_copy(amp.at[c - k * tiles], abuf.at[s], asem.at[g]).start()

            @pl.when(jnp.logical_not(mine))
            def _():
                pltpu.make_async_copy(halo.at[c + shift * tiles], abuf.at[s], asem.at[g]).start()


    def start_blocks(g, carry):
        block_copy(g).start()
        return carry

    block_copy(0).start()
    fetch(0)
    lax.fori_loop(1, groups, start_blocks, 0)
    for g in range(1, AHEAD):
        pl.when(g < groups)(functools.partial(fetch, g))
    out[...] = jnp.zeros_like(out)

    def note(p, carry):
        table[pairs[p, 0] * 128 + pairs[p, 1]] = p
        return carry

    lax.fori_loop(0, pair_count, note, 0)

    def step(g, carry):
        base = g * GROUP
        pl.when(g + AHEAD < groups)(lambda: fetch(g + AHEAD))
        pltpu.make_async_copy(
            halo.at[pl.ds(0, GROUP)], abuf.at[pl.ds(base, GROUP)], asem.at[g]
        ).wait()
        block_copy(g).wait()
        terms = []
        for i in range(GROUP):
            left = split(abuf[base + i])
            right = split(bbuf[base + i])
            full = lax.dot_general(
                left, right, (((1,), (1,)), ((), ())), preferred_element_type=jnp.float32
            )
            top, low = full[:pair_count], full[pair_count:]
            terms.append(top[:, :width] + (top[:, width:] + (low[:, :width] + low[:, width:])))
        for i in range(GROUP):
            s = g * GROUP + i
            term = jnp.where(s < live[0, 0], terms[i], 0.0).reshape(out.shape[0], out.shape[3], width)
            e = ab[0, s]
            out[:, 0, e] += term
        return carry

    lax.fori_loop(0, groups, step, 0)

    def turn(q, carry):
        for i in range(8):
            m = table[pairs[q * 8 + i, 1] * 128 + pairs[q * 8 + i, 0]]
            out[q, 1, :, i : i + 1, :] = out[m // 8, 0, :, pl.ds(m % 8, 1), :]
        return carry

    lax.fori_loop(0, pair_count // 8, turn, 0)


def slot_sums(amplitudes, halo, blocks, ab, cd, live, pair_list, tiles_ab):
    pair_count, depth = halo.shape[1:]
    slots, width = blocks.shape[:2]
    anywhere = pl.BlockSpec(memory_space=pl.ANY)
    scalars = pl.BlockSpec(memory_space=pltpu.SMEM)
    return pl.pallas_call(
        slots_kernel,
        out_shape=jax.ShapeDtypeStruct((pair_count // 8, 2, tiles_ab, 8, width), jnp.float32),
        in_specs=[anywhere] * 3 + [scalars] * 4,
        out_specs=pl.BlockSpec(memory_space=pltpu.VMEM),
        scratch_shapes=[
            pltpu.VMEM((slots, pair_count, depth), jnp.float32),
            pltpu.VMEM((slots, width, depth), jnp.float32),
            pltpu.SemaphoreType.DMA((slots // GROUP,)),
            pltpu.SemaphoreType.DMA((slots // GROUP,)),
            pltpu.SMEM((128 * 128,), jnp.int32),
        ],
        compiler_params=pltpu.CompilerParams(vmem_limit_bytes=24 * 1024 * 1024),
    )(amplitudes, halo, blocks, ab, cd, live, pair_list)


def sum_kernel(sums, ladder, turned, bx, sz, bz, mine, send_x, recv_x, send_z, recv_z, send_r, recv_r):
    k, r, z, x = place()
    other_x = (z * 2 + 1 - x, r)
    zs = [((z + i) % 4 * 2 + x, r) for i in range(1, 4)]
    rows = [(k, (r + i) % 4) for i in range(1, 4)]
    greet([other_x] + zs + rows)

    def remote(src, dst, sent, received, device):
        return pltpu.make_async_remote_copy(
            src_ref=src, dst_ref=dst, send_sem=sent, recv_sem=received, device_id=device, device_id_type=MESH
        )

    steps = [(i, h) for i in (2, 1, 3, 0) for h in range(2)]
    over_x = {
        (i, h): remote(
            sums.at[(z + i) % 4 * 2 + 1 - x, h], bx.at[i, h], send_x.at[i, h], recv_x.at[i, h], other_x
        )
        for i, h in steps
    }
    over_z = {
        (i, h): remote(sz.at[i, h], bz.at[i, h], send_z.at[i, h], recv_z.at[i, h], zs[i - 1])
        for i, h in steps if i > 0
    }
    for step in steps[:WINDOW]:
        over_x[step].start()
    for j, (i, h) in enumerate(steps):
        over_x[i, h].wait_recv()
        if j + WINDOW < len(steps):
            over_x[steps[j + WINDOW]].start()
        total = bx[i, h] + sums[(z + i) % 4 * 2 + x, h]
        if i > 0:
            sz[i, h] = total
            over_z[i, h].start()
        else:
            mine[h] = total
    for i in (1, 3, 2):
        for h in range(2):
            over_z[i, h].wait_recv()
    total = mine[...] + bz[1] + bz[2] + bz[3]
    ladder[...] = total[0].reshape(ladder.shape)
    mine[...] = total
    parts = mine.at[1]

    def over_row(i):
        first = (r + i) % 4 * 3 // 2
        return [
            remote(
                parts.at[pl.ds(t * 6 + first, 2)], turned.at[r, t], send_r.at[i, t], recv_r.at[i, t], rows[i - 1]
            )
            for t in range(3)
        ]

    copies = [c for i in range(1, 4) for c in over_row(i)]
    for c in copies:
        c.start()
    own = r * 3 // 2
    for t in range(3):
        turned[r, t] = mine[1, pl.ds(t * 6 + own, 2)]
    for i in range(1, 4):
        source = (r + 4 - i) % 4
        for t in range(3):
            remote(
                parts.at[pl.ds(0, 2)], turned.at[source, t], send_r.at[i, t], recv_r.at[i, t], rows[i - 1]
            ).wait_recv()
    for c in copies + list(over_x.values()) + list(over_z.values()):
        c.wait_send()


def sum_over_tile(sums):
    chunk = sums.shape[1:]
    vmem = pl.BlockSpec(memory_space=pltpu.VMEM)
    dma = pltpu.SemaphoreType.DMA
    return pl.pallas_call(
        sum_kernel,
        out_shape=(
            jax.ShapeDtypeStruct((3, 6) + chunk[2:], jnp.float32),
            jax.ShapeDtypeStruct((4, 3, 2) + chunk[2:], jnp.float32),
        ),
        in_specs=[vmem],
        out_specs=(vmem, vmem),
        scratch_shapes=[
            pltpu.VMEM((4,) + chunk, jnp.float32),
            pltpu.VMEM((4,) + chunk, jnp.float32),
            pltpu.VMEM((4,) + chunk, jnp.float32),
            pltpu.VMEM(chunk, jnp.float32),
            dma((4, 2)), dma((4, 2)), dma((4, 2)), dma((4, 2)), dma((4, 3)), dma((4, 3)),
        ],
        compiler_params=pltpu.CompilerParams(
            collective_id=1, has_side_effects=True, vmem_limit_bytes=16 * 1024 * 1024
        ),
    )(sums)


def shards_8x4(amplitudes, integrals, slot_ab, slot_cd, live_count, pair_list):
    halo = halo_of(amplitudes)
    sums = slot_sums(amplitudes, halo, integrals[0], slot_ab, slot_cd, live_count, pair_list, 18)
    ladder, turned = sum_over_tile(sums)
    local_pairs = ladder.shape[2]
    grid = jnp.transpose(ladder.reshape(3, 6, local_pairs, ATS, TS), (2, 0, 3, 1, 4)).reshape(local_pairs, 24, SLAB)
    other = turned.reshape(4, 3, 2, local_pairs, ATS, TS)
    other = jnp.transpose(other, (3, 2, 5, 0, 1, 4)).reshape(local_pairs, 2 * TS, SLAB)
    shift = lax.axis_index("row") % 2 * 8
    return grid + lax.dynamic_slice_in_dim(other, shift, 24, axis=1)


def solution(mesh):
    fast = mesh.shape["tile"] == 8 and mesh.shape["row"] == 4
    return jax.shard_map(
        shards_8x4 if fast else shards,
        mesh=mesh,
        in_specs=(
            P("tile", None, None),
            P("row", "tile", None, None),
            P("row", "tile"),
            P("row", "tile"),
            P("row", "tile"),
            P(),
        ),
        out_specs=P("tile", "row", None),
        check_vma=False,
    )
```

```python
import functools

import jax
import jax.numpy as jnp
from jax import lax
from jax.experimental import pallas as pl
from jax.experimental.pallas import tpu as pltpu
from jax.sharding import PartitionSpec as P

TS = 16
ATS = 8
SLAB = 96


def padded(x, sides, width):
    for axis, dim in sides:
        size, length = (lax.axis_size(axis), x.shape[dim])
        up = [(i, (i + 1) % size) for i in range(size)]
        down = [(j, i) for i, j in up]
        last = lax.slice_in_dim(x, length - width, length, axis=dim)
        first = lax.slice_in_dim(x, 0, width, axis=dim)
        before = lax.ppermute(last, axis, up)
        after = lax.ppermute(first, axis, down)
        x = jnp.concatenate([before, x, after], axis=dim)
    return x


def find_mirror(pair_list):
    first_orb = pair_list[:, 0]
    second = pair_list[:, 1]
    matches = (first_orb[:, None] == second[None, :]) & (second[:, None] == first_orb[None, :])
    columns = jnp.arange(pair_list.shape[0], dtype=jnp.int32)
    return jnp.sum(jnp.where(matches, columns[None, :], 0), axis=1)


def to_grid(totals, a_tiles, b_tiles):
    pair_count = totals.shape[1]
    shaped = totals.reshape(a_tiles, b_tiles, pair_count, ATS, TS)
    return jnp.transpose(shaped, (2, 0, 3, 1, 4)).reshape(pair_count, a_tiles * ATS, b_tiles * TS)


def shards(amplitudes, integrals, slot_ab, slot_cd, live_count, pair_list):
    highest = lax.Precision.HIGHEST
    tile_size = lax.axis_size("tile")
    row_size = lax.axis_size("row")
    tile_index = lax.axis_index("tile")
    shard_tiles = amplitudes.shape[0]
    pair_count = amplitudes.shape[1]
    extended = padded(amplitudes, (("tile", 0),), shard_tiles)
    blocks_all = integrals[0]
    ab_local = slot_ab[0]
    cd_global = slot_cd[0]
    owner_tile = cd_global // shard_tiles
    offset = (owner_tile - tile_index + 1 + tile_size) % tile_size
    ext_index = offset * shard_tiles + cd_global % shard_tiles
    live_total = live_count[0, 0]
    a_tiles = SLAB // (row_size * ATS)
    b_tiles = SLAB // TS
    tiles_ab = a_tiles * b_tiles
    block_width = integrals.shape[2]
    group_size = 8

    def block_step(block_index, totals):
        first_slot = block_index * group_size
        picked = lax.dynamic_slice_in_dim(ext_index, first_slot, group_size)
        ab_tiles = lax.dynamic_slice_in_dim(ab_local, first_slot, group_size)
        blocks = lax.dynamic_slice_in_dim(blocks_all, first_slot, group_size, 0)
        live_mask = (first_slot + jnp.arange(group_size, dtype=jnp.int32) < live_total).astype(
            jnp.float32
        )
        amp_tiles = jnp.take(extended, picked, axis=0)
        products = jnp.einsum(
            "spw,sbw->spb", amp_tiles, blocks, precision=highest, preferred_element_type=jnp.float32
        )
        one_hot = (ab_tiles[:, None] == jnp.arange(tiles_ab, dtype=jnp.int32)[None, :]).astype(
            jnp.float32
        ) * live_mask[:, None]
        return totals + jnp.einsum(
            "se,spb->epb", one_hot, products, precision=highest, preferred_element_type=jnp.float32
        )

    turn_count = (live_total + group_size - 1) // group_size
    start_totals = jnp.zeros((tiles_ab, pair_count, block_width), jnp.float32)
    totals = lax.fori_loop(0, turn_count, block_step, start_totals)
    whole_term = to_grid(totals, a_tiles, b_tiles)
    mirror = find_mirror(pair_list)
    reduced = lax.psum_scatter(whole_term, "tile", scatter_dimension=0, tiled=True)
    exchanged = lax.all_to_all(reduced, "row", split_axis=2, concat_axis=1, tiled=True)
    turned = jnp.transpose(exchanged, (0, 2, 1))
    everyone = lax.all_gather(turned, "tile", axis=0, tiled=True)
    local_pairs = reduced.shape[0]
    wanted = lax.dynamic_slice_in_dim(mirror, tile_index * local_pairs, local_pairs)
    return reduced + jnp.take(everyone, wanted, axis=0)


MESH = pl.DeviceIdType.MESH
CHUNK = 2
WINDOW = 4
GROUP = 8
AHEAD = 2
VMEM_BYTES = 56 * 1024 * 1024


def place():
    k = lax.axis_index("tile")
    r = lax.axis_index("row")
    return k, r, k // 2, k % 2


def greet(devices):
    barrier = pltpu.get_barrier_semaphore()
    for device in devices:
        pl.semaphore_signal(barrier, inc=1, device_id=device, device_id_type=MESH)
    pl.semaphore_wait(barrier, len(devices))


def halo_kernel(tiles, amp, halo, send, rx, rz, ry, rc):
    k, r, z, x = place()
    y, core = r // 2, r % 2
    sixth = tiles // 6
    half = sixth // CHUNK
    count = 2 * half
    other_x = (z * 2 + 1 - x, r)
    up = ((z + 1) % 4 * 2 + x, r)
    down = ((z + 3) % 4 * 2 + x, r)
    next_z = (jnp.where(x == 0, up[0], down[0]), r)
    other_y = (k, (1 - y) * 2 + core)
    other_core = (k, y * 2 + 1 - core)
    greet((other_x, up, down, other_y, other_core))

    def first_of(yy, cc, j):
        own = (yy * 2 + cc) * sixth + j * CHUNK
        both = (4 + cc) * sixth + (j - half) * CHUNK
        return own if j < half else both

    def remote(src, dst, sent, received, device):
        return pltpu.make_async_remote_copy(
            src_ref=src, dst_ref=dst, send_sem=sent, recv_sem=received, device_id=device, device_id_type=MESH
        )

    def at(side, first):
        return halo.at[pl.ds(side * tiles + first, CHUNK)]

    def copy_x(j):
        first = first_of(y, core, j)
        return remote(amp.at[pl.ds(first, CHUNK)], at(0, first), send.at[0, j], rx.at[j], other_x)

    def copy_z(j):
        first = first_of(y, core, j)
        return remote(at(0, first), at(1, first), send.at[1, j], rz.at[j], next_z)

    def copy_y(side, j):
        first = first_of(y, core, j)
        return remote(at(side, first), at(side, first), send.at[2 + side, j], ry.at[side, j], other_y)

    def copy_c(side, j):
        first = first_of(y, core, j) if j < count else first_of(1 - y, core, j - count)
        return remote(at(side, first), at(side, first), send.at[4 + side, j], rc.at[side, j], other_core)

    sends = []

    def go(copy):
        copy.start()
        sends.append(copy)

    for j in range(WINDOW):
        go(copy_x(j))
    lag = 1
    for i in range(count + 3 * lag):
        if i < count:
            copy_x(i).wait_recv()
            if i + WINDOW < count:
                go(copy_x(i + WINDOW))
            go(copy_z(i))
            if i < half:
                go(copy_y(0, i))
            go(copy_c(0, i))
        j = i - lag
        if 0 <= j < count:
            copy_z(j).wait_recv()
            if j < half:
                go(copy_y(1, j))
            go(copy_c(1, j))
        j = i - 2 * lag
        if 0 <= j < half:
            copy_y(0, j).wait_recv()
            go(copy_c(0, count + j))
        j = i - 3 * lag
        if 0 <= j < half:
            copy_y(1, j).wait_recv()
            go(copy_c(1, count + j))
    for j in range(count + half):
        for side in range(2):
            copy_c(side, j).wait_recv()
    for copy in sends:
        copy.wait_send()


def halo_of(amplitudes):
    tiles = amplitudes.shape[0]
    count = tiles // 3 // CHUNK
    return pl.pallas_call(
        functools.partial(halo_kernel, tiles),
        out_shape=jax.ShapeDtypeStruct((2 * tiles,) + amplitudes.shape[1:], jnp.float32),
        in_specs=[pl.BlockSpec(memory_space=pl.ANY)],
        out_specs=pl.BlockSpec(memory_space=pl.ANY),
        scratch_shapes=[
            pltpu.SemaphoreType.DMA((6, count + count // 2)),
            pltpu.SemaphoreType.DMA((count,)),
            pltpu.SemaphoreType.DMA((count,)),
            pltpu.SemaphoreType.DMA((2, count // 2)),
            pltpu.SemaphoreType.DMA((2, count + count // 2)),
        ],
        compiler_params=pltpu.CompilerParams(
            collective_id=0, has_side_effects=True, vmem_limit_bytes=VMEM_BYTES
        ),
    )(amplitudes)


def split(v):
    high = v.astype(jnp.bfloat16)
    low = (v - high.astype(jnp.float32)).astype(jnp.bfloat16)
    return jnp.concatenate([high, low], axis=0)


def slots_kernel(amp, halo, blocks, ab, cd, live, pairs, out, abuf, bbuf, asem, bsem, table):
    k = lax.axis_index("tile")
    tiles = amp.shape[0]
    pair_count = halo.shape[1]
    width = blocks.shape[1]
    groups = (live[0, 0] + GROUP - 1) // GROUP
    x = k % 2
    other_x = k + 1 - 2 * x
    next_z = lax.rem(k + 7 + 2 * x, 8)

    def block_copy(g):
        return pltpu.make_async_copy(
            blocks.at[pl.ds(g * GROUP, GROUP)], bbuf.at[pl.ds(g * GROUP, GROUP)], bsem.at[g]
        )

    def fetch(g):
        for i in range(GROUP):
            s = g * GROUP + i
            c = cd[0, s]
            mine = (c >= k * tiles) & (c < (k + 1) * tiles)
            beside = (c >= other_x * tiles) & (c < (other_x + 1) * tiles)
            shift = jnp.where(beside, -other_x, 1 - next_z)

            @pl.when(mine)
            def _():
                pltpu.make_async_copy(amp.at[c - k * tiles], abuf.at[s], asem.at[g]).start()

            @pl.when(jnp.logical_not(mine))
            def _():
                pltpu.make_async_copy(halo.at[c + shift * tiles], abuf.at[s], asem.at[g]).start()


    def start_blocks(g, carry):
        block_copy(g).start()
        return carry

    block_copy(0).start()
    fetch(0)
    lax.fori_loop(1, groups, start_blocks, 0)
    for g in range(1, AHEAD):
        pl.when(g < groups)(functools.partial(fetch, g))
    out[...] = jnp.zeros_like(out)

    def note(p, carry):
        table[pairs[p, 0] * 128 + pairs[p, 1]] = p
        return carry

    lax.fori_loop(0, pair_count, note, 0)

    def step(g, carry):
        base = g * GROUP
        pl.when(g + AHEAD < groups)(lambda: fetch(g + AHEAD))
        pltpu.make_async_copy(
            halo.at[pl.ds(0, GROUP)], abuf.at[pl.ds(base, GROUP)], asem.at[g]
        ).wait()
        block_copy(g).wait()
        terms = []
        for i in range(GROUP):
            left = split(abuf[base + i])
            right = split(bbuf[base + i])
            full = lax.dot_general(
                left, right, (((1,), (1,)), ((), ())), preferred_element_type=jnp.float32
            )
            top, low = full[:pair_count], full[pair_count:]
            terms.append(top[:, :width] + (top[:, width:] + (low[:, :width] + low[:, width:])))
        for i in range(GROUP):
            s = g * GROUP + i
            term = jnp.where(s < live[0, 0], terms[i], 0.0).reshape(out.shape[0], out.shape[3], width)
            e = ab[0, s]
            out[:, 0, e] += term
        return carry

    lax.fori_loop(0, groups, step, 0)

    def turn(q, carry):
        for i in range(8):
            m = table[pairs[q * 8 + i, 1] * 128 + pairs[q * 8 + i, 0]]
            out[q, 1, :, i : i + 1, :] = out[m // 8, 0, :, pl.ds(m % 8, 1), :]
        return carry

    lax.fori_loop(0, pair_count // 8, turn, 0)


def slot_sums(amplitudes, halo, blocks, ab, cd, live, pair_list, tiles_ab):
    pair_count, depth = halo.shape[1:]
    slots, width = blocks.shape[:2]
    anywhere = pl.BlockSpec(memory_space=pl.ANY)
    scalars = pl.BlockSpec(memory_space=pltpu.SMEM)
    return pl.pallas_call(
        slots_kernel,
        out_shape=jax.ShapeDtypeStruct((pair_count // 8, 2, tiles_ab, 8, width), jnp.float32),
        in_specs=[anywhere] * 3 + [scalars] * 4,
        out_specs=pl.BlockSpec(memory_space=pltpu.VMEM),
        scratch_shapes=[
            pltpu.VMEM((slots, pair_count, depth), jnp.float32),
            pltpu.VMEM((slots, width, depth), jnp.float32),
            pltpu.SemaphoreType.DMA((slots // GROUP,)),
            pltpu.SemaphoreType.DMA((slots // GROUP,)),
            pltpu.SMEM((128 * 128,), jnp.int32),
        ],
        compiler_params=pltpu.CompilerParams(vmem_limit_bytes=VMEM_BYTES),
    )(amplitudes, halo, blocks, ab, cd, live, pair_list)


def sum_kernel(sums, ladder, turned, bx, sz, bz, mine, send_x, recv_x, send_z, recv_z, send_r, recv_r):
    k, r, z, x = place()
    other_x = (z * 2 + 1 - x, r)
    zs = [((z + i) % 4 * 2 + x, r) for i in range(1, 4)]
    rows = [(k, (r + i) % 4) for i in range(1, 4)]
    greet([other_x] + zs + rows)

    def remote(src, dst, sent, received, device):
        return pltpu.make_async_remote_copy(
            src_ref=src, dst_ref=dst, send_sem=sent, recv_sem=received, device_id=device, device_id_type=MESH
        )

    steps = [(i, h) for h in (1, 0) for i in (2, 1, 3, 0)]
    over_x = {
        (i, h): remote(
            sums.at[(z + i) % 4 * 2 + 1 - x, h], bx.at[i, h], send_x.at[i, h], recv_x.at[i, h], other_x
        )
        for i, h in steps
    }
    over_z = {
        (i, h): remote(sz.at[i, h], bz.at[i, h], send_z.at[i, h], recv_z.at[i, h], zs[i - 1])
        for i, h in steps if i > 0
    }
    for step in steps[:WINDOW]:
        over_x[step].start()
    for j, (i, h) in enumerate(steps):
        over_x[i, h].wait_recv()
        if j + WINDOW < len(steps):
            over_x[steps[j + WINDOW]].start()
        total = bx[i, h] + sums[(z + i) % 4 * 2 + x, h]
        if i > 0:
            sz[i, h] = total
            over_z[i, h].start()
        else:
            mine[h] = total
    def finish(h):
        for i in (1, 3, 2):
            over_z[i, h].wait_recv()
        return mine[h] + bz[1, h] + bz[2, h] + bz[3, h]

    mine[1] = finish(1)
    parts = mine.at[1]

    def over_row(i):
        first = (r + i) % 4 * 3 // 2
        return [
            remote(
                parts.at[pl.ds(t * 6 + first, 2)], turned.at[r, t], send_r.at[i, t], recv_r.at[i, t], rows[i - 1]
            )
            for t in range(3)
        ]

    copies = [c for i in range(1, 4) for c in over_row(i)]
    for c in copies:
        c.start()
    own = r * 3 // 2
    for t in range(3):
        turned[r, t] = mine[1, pl.ds(t * 6 + own, 2)]
    ladder[...] = finish(0).reshape(ladder.shape)
    for i in range(1, 4):
        source = (r + 4 - i) % 4
        for t in range(3):
            remote(
                parts.at[pl.ds(0, 2)], turned.at[source, t], send_r.at[i, t], recv_r.at[i, t], rows[i - 1]
            ).wait_recv()
    for c in copies + list(over_x.values()) + list(over_z.values()):
        c.wait_send()


def sum_over_tile(sums):
    chunk = sums.shape[1:]
    vmem = pl.BlockSpec(memory_space=pltpu.VMEM)
    dma = pltpu.SemaphoreType.DMA
    return pl.pallas_call(
        sum_kernel,
        out_shape=(
            jax.ShapeDtypeStruct((3, 6) + chunk[2:], jnp.float32),
            jax.ShapeDtypeStruct((4, 3, 2) + chunk[2:], jnp.float32),
        ),
        in_specs=[vmem],
        out_specs=(vmem, vmem),
        scratch_shapes=[
            pltpu.VMEM((4,) + chunk, jnp.float32),
            pltpu.VMEM((4,) + chunk, jnp.float32),
            pltpu.VMEM((4,) + chunk, jnp.float32),
            pltpu.VMEM(chunk, jnp.float32),
            dma((4, 2)), dma((4, 2)), dma((4, 2)), dma((4, 2)), dma((4, 3)), dma((4, 3)),
        ],
        compiler_params=pltpu.CompilerParams(
            collective_id=1, has_side_effects=True, vmem_limit_bytes=16 * 1024 * 1024
        ),
    )(sums)


def shards_8x4(amplitudes, integrals, slot_ab, slot_cd, live_count, pair_list):
    halo = halo_of(amplitudes)
    sums = slot_sums(amplitudes, halo, integrals[0], slot_ab, slot_cd, live_count, pair_list, 18)
    ladder, turned = sum_over_tile(sums)
    local_pairs = ladder.shape[2]
    grid = jnp.transpose(ladder.reshape(3, 6, local_pairs, ATS, TS), (2, 0, 3, 1, 4)).reshape(local_pairs, 24, SLAB)
    other = turned.reshape(4, 3, 2, local_pairs, ATS, TS)
    other = jnp.transpose(other, (3, 2, 5, 0, 1, 4)).reshape(local_pairs, 2 * TS, SLAB)
    shift = lax.axis_index("row") % 2 * 8
    return grid + lax.dynamic_slice_in_dim(other, shift, 24, axis=1)


def solution(mesh):
    fast = mesh.shape["tile"] == 8 and mesh.shape["row"] == 4
    return jax.shard_map(
        shards_8x4 if fast else shards,
        mesh=mesh,
        in_specs=(
            P("tile", None, None),
            P("row", "tile", None, None),
            P("row", "tile"),
            P("row", "tile"),
            P("row", "tile"),
            P(),
        ),
        out_specs=P("tile", "row", None),
        check_vma=False,
    )
```

```python
import functools

import jax
import jax.numpy as jnp
from jax import lax
from jax.experimental import pallas as pl
from jax.experimental.pallas import tpu as pltpu
from jax.sharding import PartitionSpec as P

TS = 16
ATS = 8
SLAB = 96


def padded(x, sides, width):
    for axis, dim in sides:
        size, length = (lax.axis_size(axis), x.shape[dim])
        up = [(i, (i + 1) % size) for i in range(size)]
        down = [(j, i) for i, j in up]
        last = lax.slice_in_dim(x, length - width, length, axis=dim)
        first = lax.slice_in_dim(x, 0, width, axis=dim)
        before = lax.ppermute(last, axis, up)
        after = lax.ppermute(first, axis, down)
        x = jnp.concatenate([before, x, after], axis=dim)
    return x


def find_mirror(pair_list):
    first_orb = pair_list[:, 0]
    second = pair_list[:, 1]
    matches = (first_orb[:, None] == second[None, :]) & (second[:, None] == first_orb[None, :])
    columns = jnp.arange(pair_list.shape[0], dtype=jnp.int32)
    return jnp.sum(jnp.where(matches, columns[None, :], 0), axis=1)


def to_grid(totals, a_tiles, b_tiles):
    pair_count = totals.shape[1]
    shaped = totals.reshape(a_tiles, b_tiles, pair_count, ATS, TS)
    return jnp.transpose(shaped, (2, 0, 3, 1, 4)).reshape(pair_count, a_tiles * ATS, b_tiles * TS)


def shards(amplitudes, integrals, slot_ab, slot_cd, live_count, pair_list):
    highest = lax.Precision.HIGHEST
    tile_size = lax.axis_size("tile")
    row_size = lax.axis_size("row")
    tile_index = lax.axis_index("tile")
    shard_tiles = amplitudes.shape[0]
    pair_count = amplitudes.shape[1]
    extended = padded(amplitudes, (("tile", 0),), shard_tiles)
    blocks_all = integrals[0]
    ab_local = slot_ab[0]
    cd_global = slot_cd[0]
    owner_tile = cd_global // shard_tiles
    offset = (owner_tile - tile_index + 1 + tile_size) % tile_size
    ext_index = offset * shard_tiles + cd_global % shard_tiles
    live_total = live_count[0, 0]
    a_tiles = SLAB // (row_size * ATS)
    b_tiles = SLAB // TS
    tiles_ab = a_tiles * b_tiles
    block_width = integrals.shape[2]
    group_size = 8

    def block_step(block_index, totals):
        first_slot = block_index * group_size
        picked = lax.dynamic_slice_in_dim(ext_index, first_slot, group_size)
        ab_tiles = lax.dynamic_slice_in_dim(ab_local, first_slot, group_size)
        blocks = lax.dynamic_slice_in_dim(blocks_all, first_slot, group_size, 0)
        live_mask = (first_slot + jnp.arange(group_size, dtype=jnp.int32) < live_total).astype(
            jnp.float32
        )
        amp_tiles = jnp.take(extended, picked, axis=0)
        products = jnp.einsum(
            "spw,sbw->spb", amp_tiles, blocks, precision=highest, preferred_element_type=jnp.float32
        )
        one_hot = (ab_tiles[:, None] == jnp.arange(tiles_ab, dtype=jnp.int32)[None, :]).astype(
            jnp.float32
        ) * live_mask[:, None]
        return totals + jnp.einsum(
            "se,spb->epb", one_hot, products, precision=highest, preferred_element_type=jnp.float32
        )

    turn_count = (live_total + group_size - 1) // group_size
    start_totals = jnp.zeros((tiles_ab, pair_count, block_width), jnp.float32)
    totals = lax.fori_loop(0, turn_count, block_step, start_totals)
    whole_term = to_grid(totals, a_tiles, b_tiles)
    mirror = find_mirror(pair_list)
    reduced = lax.psum_scatter(whole_term, "tile", scatter_dimension=0, tiled=True)
    exchanged = lax.all_to_all(reduced, "row", split_axis=2, concat_axis=1, tiled=True)
    turned = jnp.transpose(exchanged, (0, 2, 1))
    everyone = lax.all_gather(turned, "tile", axis=0, tiled=True)
    local_pairs = reduced.shape[0]
    wanted = lax.dynamic_slice_in_dim(mirror, tile_index * local_pairs, local_pairs)
    return reduced + jnp.take(everyone, wanted, axis=0)


MESH = pl.DeviceIdType.MESH
CHUNK = 1
WINDOW = 8
GROUP = 8
AHEAD = 2
VMEM_BYTES = 56 * 1024 * 1024


def place():
    k = lax.axis_index("tile")
    r = lax.axis_index("row")
    return k, r, k // 2, k % 2


def greet(devices):
    barrier = pltpu.get_barrier_semaphore()
    for device in devices:
        pl.semaphore_signal(barrier, inc=1, device_id=device, device_id_type=MESH)
    pl.semaphore_wait(barrier, len(devices))


def halo_kernel(tiles, amp, halo, send, rx, rz, ry, rc):
    k, r, z, x = place()
    y, core = r // 2, r % 2
    sixth = tiles // 6
    half = sixth // CHUNK
    count = 2 * half
    other_x = (z * 2 + 1 - x, r)
    up = ((z + 1) % 4 * 2 + x, r)
    down = ((z + 3) % 4 * 2 + x, r)
    next_z = (jnp.where(x == 0, up[0], down[0]), r)
    other_y = (k, (1 - y) * 2 + core)
    other_core = (k, y * 2 + 1 - core)
    greet((other_x, up, down, other_y, other_core))

    def first_of(yy, cc, j):
        own = (yy * 2 + cc) * sixth + j * CHUNK
        both = (4 + cc) * sixth + (j - half) * CHUNK
        return own if j < half else both

    def remote(src, dst, sent, received, device):
        return pltpu.make_async_remote_copy(
            src_ref=src, dst_ref=dst, send_sem=sent, recv_sem=received, device_id=device, device_id_type=MESH
        )

    def at(side, first):
        return halo.at[pl.ds(side * tiles + first, CHUNK)]

    def copy_x(j):
        first = first_of(y, core, j)
        return remote(amp.at[pl.ds(first, CHUNK)], at(0, first), send.at[0, j], rx.at[j], other_x)

    def copy_z(j):
        first = first_of(y, core, j)
        return remote(at(0, first), at(1, first), send.at[1, j], rz.at[j], next_z)

    def copy_y(side, j):
        first = first_of(y, core, j)
        return remote(at(side, first), at(side, first), send.at[2 + side, j], ry.at[side, j], other_y)

    def copy_c(side, j):
        first = first_of(y, core, j) if j < count else first_of(1 - y, core, j - count)
        return remote(at(side, first), at(side, first), send.at[4 + side, j], rc.at[side, j], other_core)

    sends = []

    def go(copy):
        copy.start()
        sends.append(copy)

    for j in range(WINDOW):
        go(copy_x(j))
    lag = 2
    for i in range(count + 3 * lag):
        if i < count:
            copy_x(i).wait_recv()
            if i + WINDOW < count:
                go(copy_x(i + WINDOW))
            go(copy_z(i))
            if i < half:
                go(copy_y(0, i))
            go(copy_c(0, i))
        j = i - lag
        if 0 <= j < count:
            copy_z(j).wait_recv()
            if j < half:
                go(copy_y(1, j))
            go(copy_c(1, j))
        j = i - 2 * lag
        if 0 <= j < half:
            copy_y(0, j).wait_recv()
            go(copy_c(0, count + j))
        j = i - 3 * lag
        if 0 <= j < half:
            copy_y(1, j).wait_recv()
            go(copy_c(1, count + j))
    for j in range(count + half):
        for side in range(2):
            copy_c(side, j).wait_recv()
    for copy in sends:
        copy.wait_send()


def halo_of(amplitudes):
    tiles = amplitudes.shape[0]
    count = tiles // 3 // CHUNK
    return pl.pallas_call(
        functools.partial(halo_kernel, tiles),
        out_shape=jax.ShapeDtypeStruct((2 * tiles,) + amplitudes.shape[1:], jnp.float32),
        in_specs=[pl.BlockSpec(memory_space=pl.ANY)],
        out_specs=pl.BlockSpec(memory_space=pl.ANY),
        scratch_shapes=[
            pltpu.SemaphoreType.DMA((6, count + count // 2)),
            pltpu.SemaphoreType.DMA((count,)),
            pltpu.SemaphoreType.DMA((count,)),
            pltpu.SemaphoreType.DMA((2, count // 2)),
            pltpu.SemaphoreType.DMA((2, count + count // 2)),
        ],
        compiler_params=pltpu.CompilerParams(
            collective_id=0, has_side_effects=True, vmem_limit_bytes=VMEM_BYTES
        ),
    )(amplitudes)


def split(v):
    high = v.astype(jnp.bfloat16)
    low = (v - high.astype(jnp.float32)).astype(jnp.bfloat16)
    return jnp.concatenate([high, low], axis=0)


def slots_kernel(amp, halo, blocks, ab, cd, live, pairs, out, abuf, bbuf, asem, bsem, table):
    k = lax.axis_index("tile")
    tiles = amp.shape[0]
    pair_count = halo.shape[1]
    width = blocks.shape[1]
    groups = (live[0, 0] + GROUP - 1) // GROUP
    x = k % 2
    other_x = k + 1 - 2 * x
    next_z = lax.rem(k + 7 + 2 * x, 8)

    def block_copy(g):
        return pltpu.make_async_copy(
            blocks.at[pl.ds(g * GROUP, GROUP)], bbuf.at[pl.ds(g * GROUP, GROUP)], bsem.at[g]
        )

    def fetch(g):
        for i in range(GROUP):
            s = g * GROUP + i
            c = cd[0, s]
            mine = (c >= k * tiles) & (c < (k + 1) * tiles)
            beside = (c >= other_x * tiles) & (c < (other_x + 1) * tiles)
            shift = jnp.where(beside, -other_x, 1 - next_z)

            @pl.when(mine)
            def _():
                pltpu.make_async_copy(amp.at[c - k * tiles], abuf.at[s], asem.at[g]).start()

            @pl.when(jnp.logical_not(mine))
            def _():
                pltpu.make_async_copy(halo.at[c + shift * tiles], abuf.at[s], asem.at[g]).start()


    def start_blocks(g, carry):
        block_copy(g).start()
        return carry

    block_copy(0).start()
    fetch(0)
    lax.fori_loop(1, groups, start_blocks, 0)
    for g in range(1, AHEAD):
        pl.when(g < groups)(functools.partial(fetch, g))
    out[...] = jnp.zeros_like(out)

    def note(p, carry):
        table[pairs[0, p] * 128 + pairs[1, p]] = p
        return carry

    lax.fori_loop(0, pair_count, note, 0)

    def step(g, carry):
        base = g * GROUP
        pl.when(g + AHEAD < groups)(lambda: fetch(g + AHEAD))
        pltpu.make_async_copy(
            halo.at[pl.ds(0, GROUP)], abuf.at[pl.ds(base, GROUP)], asem.at[g]
        ).wait()
        block_copy(g).wait()
        terms = []
        for i in range(GROUP):
            left = split(abuf[base + i])
            right = split(bbuf[base + i])
            full = lax.dot_general(
                left, right, (((1,), (1,)), ((), ())), preferred_element_type=jnp.float32
            )
            top, low = full[:pair_count], full[pair_count:]
            terms.append(top[:, :width] + (top[:, width:] + (low[:, :width] + low[:, width:])))
        for i in range(GROUP):
            s = g * GROUP + i
            term = jnp.where(s < live[0, 0], terms[i], 0.0).reshape(out.shape[0], out.shape[3], width)
            e = ab[0, s]
            out[:, 0, e] += term
        return carry

    lax.fori_loop(0, groups, step, 0)

    def turn(q, carry):
        for i in range(8):
            m = table[pairs[1, q * 8 + i] * 128 + pairs[0, q * 8 + i]]
            out[q, 1, :, i : i + 1, :] = out[m // 8, 0, :, pl.ds(m % 8, 1), :]
        return carry

    lax.fori_loop(0, pair_count // 8, turn, 0)


def slot_sums(amplitudes, halo, blocks, ab, cd, live, pair_list, tiles_ab):
    pair_count, depth = halo.shape[1:]
    slots, width = blocks.shape[:2]
    anywhere = pl.BlockSpec(memory_space=pl.ANY)
    scalars = pl.BlockSpec(memory_space=pltpu.SMEM)
    return pl.pallas_call(
        slots_kernel,
        out_shape=jax.ShapeDtypeStruct((pair_count // 8, 2, tiles_ab, 8, width), jnp.float32),
        in_specs=[anywhere] * 3 + [scalars] * 4,
        out_specs=pl.BlockSpec(memory_space=pltpu.VMEM),
        scratch_shapes=[
            pltpu.VMEM((slots, pair_count, depth), jnp.float32),
            pltpu.VMEM((slots, width, depth), jnp.float32),
            pltpu.SemaphoreType.DMA((slots // GROUP,)),
            pltpu.SemaphoreType.DMA((slots // GROUP,)),
            pltpu.SMEM((128 * 128,), jnp.int32),
        ],
        compiler_params=pltpu.CompilerParams(vmem_limit_bytes=VMEM_BYTES),
    )(amplitudes, halo, blocks, ab, cd, live, pair_list)


def sum_kernel(sums, ladder, turned, bx, sz, bz, mine, send_x, recv_x, send_z, recv_z, send_r, recv_r):
    k, r, z, x = place()
    other_x = (z * 2 + 1 - x, r)
    zs = [((z + i) % 4 * 2 + x, r) for i in range(1, 4)]
    rows = [(k, (r + i) % 4) for i in range(1, 4)]
    greet([other_x] + zs + rows)

    def remote(src, dst, sent, received, device):
        return pltpu.make_async_remote_copy(
            src_ref=src, dst_ref=dst, send_sem=sent, recv_sem=received, device_id=device, device_id_type=MESH
        )

    steps = [(i, h) for h in (1, 0) for i in (2, 1, 3, 0)]
    over_x = {
        (i, h): remote(
            sums.at[(z + i) % 4 * 2 + 1 - x, h], bx.at[i, h], send_x.at[i, h], recv_x.at[i, h], other_x
        )
        for i, h in steps
    }
    over_z = {
        (i, h): remote(sz.at[i, h], bz.at[i, h], send_z.at[i, h], recv_z.at[i, h], zs[i - 1])
        for i, h in steps if i > 0
    }
    for step in steps[: WINDOW // 2]:
        over_x[step].start()
    for j, (i, h) in enumerate(steps):
        over_x[i, h].wait_recv()
        if j + WINDOW // 2 < len(steps):
            over_x[steps[j + WINDOW // 2]].start()
        total = bx[i, h] + sums[(z + i) % 4 * 2 + x, h]
        if i > 0:
            sz[i, h] = total
            over_z[i, h].start()
        else:
            mine[h] = total
    def finish(h):
        for i in (1, 3, 2):
            over_z[i, h].wait_recv()
        return mine[h] + bz[1, h] + bz[2, h] + bz[3, h]

    mine[1] = finish(1)
    parts = mine.at[1]

    def over_row(i):
        first = (r + i) % 4 * 3 // 2
        return [
            remote(
                parts.at[pl.ds(t * 6 + first, 2)], turned.at[r, t], send_r.at[i, t], recv_r.at[i, t], rows[i - 1]
            )
            for t in range(3)
        ]

    copies = [c for i in range(1, 4) for c in over_row(i)]
    for c in copies:
        c.start()
    own = r * 3 // 2
    for t in range(3):
        turned[r, t] = mine[1, pl.ds(t * 6 + own, 2)]
    ladder[...] = finish(0).reshape(ladder.shape)
    for i in range(1, 4):
        source = (r + 4 - i) % 4
        for t in range(3):
            remote(
                parts.at[pl.ds(0, 2)], turned.at[source, t], send_r.at[i, t], recv_r.at[i, t], rows[i - 1]
            ).wait_recv()
    for c in copies + list(over_x.values()) + list(over_z.values()):
        c.wait_send()


def sum_over_tile(sums):
    chunk = sums.shape[1:]
    vmem = pl.BlockSpec(memory_space=pltpu.VMEM)
    dma = pltpu.SemaphoreType.DMA
    return pl.pallas_call(
        sum_kernel,
        out_shape=(
            jax.ShapeDtypeStruct((3, 6) + chunk[2:], jnp.float32),
            jax.ShapeDtypeStruct((4, 3, 2) + chunk[2:], jnp.float32),
        ),
        in_specs=[vmem],
        out_specs=(vmem, vmem),
        scratch_shapes=[
            pltpu.VMEM((4,) + chunk, jnp.float32),
            pltpu.VMEM((4,) + chunk, jnp.float32),
            pltpu.VMEM((4,) + chunk, jnp.float32),
            pltpu.VMEM(chunk, jnp.float32),
            dma((4, 2)), dma((4, 2)), dma((4, 2)), dma((4, 2)), dma((4, 3)), dma((4, 3)),
        ],
        compiler_params=pltpu.CompilerParams(
            collective_id=1, has_side_effects=True, vmem_limit_bytes=16 * 1024 * 1024
        ),
    )(sums)


def shards_8x4(amplitudes, integrals, slot_ab, slot_cd, live_count, pair_list):
    halo = halo_of(amplitudes)
    sums = slot_sums(amplitudes, halo, integrals[0], slot_ab, slot_cd, live_count, pair_list.T, 18)
    ladder, turned = sum_over_tile(sums)
    local_pairs = ladder.shape[2]
    grid = jnp.transpose(ladder.reshape(3, 6, local_pairs, ATS, TS), (2, 0, 3, 1, 4)).reshape(local_pairs, 24, SLAB)
    other = turned.reshape(4, 3, 2, local_pairs, ATS, TS)
    other = jnp.transpose(other, (3, 2, 5, 0, 1, 4)).reshape(local_pairs, 2 * TS, SLAB)
    shift = lax.axis_index("row") % 2 * 8
    return grid + lax.dynamic_slice_in_dim(other, shift, 24, axis=1)


def solution(mesh):
    fast = mesh.shape["tile"] == 8 and mesh.shape["row"] == 4
    return jax.shard_map(
        shards_8x4 if fast else shards,
        mesh=mesh,
        in_specs=(
            P("tile", None, None),
            P("row", "tile", None, None),
            P("row", "tile"),
            P("row", "tile"),
            P("row", "tile"),
            P(),
        ),
        out_specs=P("tile", "row", None),
        check_vma=False,
    )
```

```python
import functools

import jax
import jax.numpy as jnp
from jax import lax
from jax.experimental import pallas as pl
from jax.experimental.pallas import tpu as pltpu
from jax.sharding import PartitionSpec as P

TS = 16
ATS = 8
SLAB = 96


def padded(x, sides, width):
    for axis, dim in sides:
        size, length = (lax.axis_size(axis), x.shape[dim])
        up = [(i, (i + 1) % size) for i in range(size)]
        down = [(j, i) for i, j in up]
        last = lax.slice_in_dim(x, length - width, length, axis=dim)
        first = lax.slice_in_dim(x, 0, width, axis=dim)
        before = lax.ppermute(last, axis, up)
        after = lax.ppermute(first, axis, down)
        x = jnp.concatenate([before, x, after], axis=dim)
    return x


def find_mirror(pair_list):
    first_orb = pair_list[:, 0]
    second = pair_list[:, 1]
    matches = (first_orb[:, None] == second[None, :]) & (second[:, None] == first_orb[None, :])
    columns = jnp.arange(pair_list.shape[0], dtype=jnp.int32)
    return jnp.sum(jnp.where(matches, columns[None, :], 0), axis=1)


def to_grid(totals, a_tiles, b_tiles):
    pair_count = totals.shape[1]
    shaped = totals.reshape(a_tiles, b_tiles, pair_count, ATS, TS)
    return jnp.transpose(shaped, (2, 0, 3, 1, 4)).reshape(pair_count, a_tiles * ATS, b_tiles * TS)


def shards(amplitudes, integrals, slot_ab, slot_cd, live_count, pair_list):
    highest = lax.Precision.HIGHEST
    tile_size = lax.axis_size("tile")
    row_size = lax.axis_size("row")
    tile_index = lax.axis_index("tile")
    shard_tiles = amplitudes.shape[0]
    pair_count = amplitudes.shape[1]
    extended = padded(amplitudes, (("tile", 0),), shard_tiles)
    blocks_all = integrals[0]
    ab_local = slot_ab[0]
    cd_global = slot_cd[0]
    owner_tile = cd_global // shard_tiles
    offset = (owner_tile - tile_index + 1 + tile_size) % tile_size
    ext_index = offset * shard_tiles + cd_global % shard_tiles
    live_total = live_count[0, 0]
    a_tiles = SLAB // (row_size * ATS)
    b_tiles = SLAB // TS
    tiles_ab = a_tiles * b_tiles
    block_width = integrals.shape[2]
    group_size = 8

    def block_step(block_index, totals):
        first_slot = block_index * group_size
        picked = lax.dynamic_slice_in_dim(ext_index, first_slot, group_size)
        ab_tiles = lax.dynamic_slice_in_dim(ab_local, first_slot, group_size)
        blocks = lax.dynamic_slice_in_dim(blocks_all, first_slot, group_size, 0)
        live_mask = (first_slot + jnp.arange(group_size, dtype=jnp.int32) < live_total).astype(
            jnp.float32
        )
        amp_tiles = jnp.take(extended, picked, axis=0)
        products = jnp.einsum(
            "spw,sbw->spb", amp_tiles, blocks, precision=highest, preferred_element_type=jnp.float32
        )
        one_hot = (ab_tiles[:, None] == jnp.arange(tiles_ab, dtype=jnp.int32)[None, :]).astype(
            jnp.float32
        ) * live_mask[:, None]
        return totals + jnp.einsum(
            "se,spb->epb", one_hot, products, precision=highest, preferred_element_type=jnp.float32
        )

    turn_count = (live_total + group_size - 1) // group_size
    start_totals = jnp.zeros((tiles_ab, pair_count, block_width), jnp.float32)
    totals = lax.fori_loop(0, turn_count, block_step, start_totals)
    whole_term = to_grid(totals, a_tiles, b_tiles)
    mirror = find_mirror(pair_list)
    reduced = lax.psum_scatter(whole_term, "tile", scatter_dimension=0, tiled=True)
    exchanged = lax.all_to_all(reduced, "row", split_axis=2, concat_axis=1, tiled=True)
    turned = jnp.transpose(exchanged, (0, 2, 1))
    everyone = lax.all_gather(turned, "tile", axis=0, tiled=True)
    local_pairs = reduced.shape[0]
    wanted = lax.dynamic_slice_in_dim(mirror, tile_index * local_pairs, local_pairs)
    return reduced + jnp.take(everyone, wanted, axis=0)


MESH = pl.DeviceIdType.MESH
CHUNK = 3
WINDOW = 4
GROUP = 8
AHEAD = 2
VMEM_BYTES = 56 * 1024 * 1024


def place():
    k = lax.axis_index("tile")
    r = lax.axis_index("row")
    return k, r, k // 2, k % 2


def greet(devices):
    barrier = pltpu.get_barrier_semaphore()
    for device in devices:
        pl.semaphore_signal(barrier, inc=1, device_id=device, device_id_type=MESH)
    pl.semaphore_wait(barrier, len(devices))


def halo_kernel(tiles, amp, halo, send, rx, rz, ry, rc):
    k, r, z, x = place()
    y, core = r // 2, r % 2
    sixth = tiles // 6
    half = sixth // CHUNK
    count = 2 * half
    other_x = (z * 2 + 1 - x, r)
    up = ((z + 1) % 4 * 2 + x, r)
    down = ((z + 3) % 4 * 2 + x, r)
    next_z = (jnp.where(x == 0, up[0], down[0]), r)
    other_y = (k, (1 - y) * 2 + core)
    other_core = (k, y * 2 + 1 - core)
    greet((other_x, up, down, other_y, other_core))

    def first_of(yy, cc, j):
        own = (yy * 2 + cc) * sixth + j * CHUNK
        both = (4 + cc) * sixth + (j - half) * CHUNK
        return own if j < half else both

    def remote(src, dst, sent, received, device):
        return pltpu.make_async_remote_copy(
            src_ref=src, dst_ref=dst, send_sem=sent, recv_sem=received, device_id=device, device_id_type=MESH
        )

    def at(side, first):
        return halo.at[pl.ds(side * tiles + first, CHUNK)]

    def copy_x(j):
        first = first_of(y, core, j)
        return remote(amp.at[pl.ds(first, CHUNK)], at(0, first), send.at[0, j], rx.at[j], other_x)

    def copy_z(j):
        first = first_of(y, core, j)
        return remote(at(0, first), at(1, first), send.at[1, j], rz.at[j], next_z)

    def copy_y(side, j):
        first = first_of(y, core, j)
        return remote(at(side, first), at(side, first), send.at[2 + side, j], ry.at[side, j], other_y)

    def copy_c(side, j):
        first = first_of(y, core, j) if j < count else first_of(1 - y, core, j - count)
        return remote(at(side, first), at(side, first), send.at[4 + side, j], rc.at[side, j], other_core)

    sends = []

    def go(copy):
        copy.start()
        sends.append(copy)

    for j in range(WINDOW):
        go(copy_x(j))
    lag = 1
    for i in range(count + 3 * lag):
        if i < count:
            copy_x(i).wait_recv()
            if i + WINDOW < count:
                go(copy_x(i + WINDOW))
            go(copy_z(i))
            if i < half:
                go(copy_y(0, i))
            go(copy_c(0, i))
        j = i - lag
        if 0 <= j < count:
            copy_z(j).wait_recv()
            if j < half:
                go(copy_y(1, j))
            go(copy_c(1, j))
        j = i - 2 * lag
        if 0 <= j < half:
            copy_y(0, j).wait_recv()
            go(copy_c(0, count + j))
        j = i - 3 * lag
        if 0 <= j < half:
            copy_y(1, j).wait_recv()
            go(copy_c(1, count + j))
    for j in range(count + half):
        for side in range(2):
            copy_c(side, j).wait_recv()
    for copy in sends:
        copy.wait_send()


def halo_of(amplitudes):
    tiles = amplitudes.shape[0]
    count = tiles // 3 // CHUNK
    return pl.pallas_call(
        functools.partial(halo_kernel, tiles),
        out_shape=jax.ShapeDtypeStruct((2 * tiles,) + amplitudes.shape[1:], jnp.float32),
        in_specs=[pl.BlockSpec(memory_space=pl.ANY)],
        out_specs=pl.BlockSpec(memory_space=pl.ANY),
        scratch_shapes=[
            pltpu.SemaphoreType.DMA((6, count + count // 2)),
            pltpu.SemaphoreType.DMA((count,)),
            pltpu.SemaphoreType.DMA((count,)),
            pltpu.SemaphoreType.DMA((2, count // 2)),
            pltpu.SemaphoreType.DMA((2, count + count // 2)),
        ],
        compiler_params=pltpu.CompilerParams(
            collective_id=0, has_side_effects=True, vmem_limit_bytes=VMEM_BYTES
        ),
    )(amplitudes)


def split(v):
    high = v.astype(jnp.bfloat16)
    low = (v - high.astype(jnp.float32)).astype(jnp.bfloat16)
    return jnp.concatenate([high, low], axis=0)


def slots_kernel(amp, halo, blocks, ab, cd, live, pairs, out, abuf, bbuf, asem, bsem, table):
    k = lax.axis_index("tile")
    tiles = amp.shape[0]
    pair_count = halo.shape[1]
    width = blocks.shape[1]
    groups = (live[0, 0] + GROUP - 1) // GROUP
    x = k % 2
    other_x = k + 1 - 2 * x
    next_z = lax.rem(k + 7 + 2 * x, 8)

    def block_copy(g):
        return pltpu.make_async_copy(
            blocks.at[pl.ds(g * GROUP, GROUP)], bbuf.at[pl.ds(g * GROUP, GROUP)], bsem.at[g]
        )

    def fetch(g):
        for i in range(GROUP):
            s = g * GROUP + i
            c = cd[0, s]
            mine = (c >= k * tiles) & (c < (k + 1) * tiles)
            beside = (c >= other_x * tiles) & (c < (other_x + 1) * tiles)
            shift = jnp.where(beside, -other_x, 1 - next_z)

            @pl.when(mine)
            def _():
                pltpu.make_async_copy(amp.at[c - k * tiles], abuf.at[s], asem.at[g]).start()

            @pl.when(jnp.logical_not(mine))
            def _():
                pltpu.make_async_copy(halo.at[c + shift * tiles], abuf.at[s], asem.at[g]).start()


    def start_blocks(g, carry):
        block_copy(g).start()
        return carry

    block_copy(0).start()
    fetch(0)
    lax.fori_loop(1, groups, start_blocks, 0)
    for g in range(1, AHEAD):
        pl.when(g < groups)(functools.partial(fetch, g))
    out[...] = jnp.zeros_like(out)

    def note(p, carry):
        table[pairs[0, p] * 128 + pairs[1, p]] = p
        return carry

    lax.fori_loop(0, pair_count, note, 0)

    def step(g, carry):
        base = g * GROUP
        pl.when(g + AHEAD < groups)(lambda: fetch(g + AHEAD))
        pltpu.make_async_copy(
            halo.at[pl.ds(0, GROUP)], abuf.at[pl.ds(base, GROUP)], asem.at[g]
        ).wait()
        block_copy(g).wait()
        terms = []
        for i in range(GROUP):
            left = split(abuf[base + i])
            right = split(bbuf[base + i])
            full = lax.dot_general(
                left, right, (((1,), (1,)), ((), ())), preferred_element_type=jnp.float32
            )
            top, low = full[:pair_count], full[pair_count:]
            terms.append(top[:, :width] + (top[:, width:] + (low[:, :width] + low[:, width:])))
        for i in range(GROUP):
            s = g * GROUP + i
            term = jnp.where(s < live[0, 0], terms[i], 0.0).reshape(out.shape[0], out.shape[3], width)
            e = ab[0, s]
            out[:, 0, e] += term
        return carry

    lax.fori_loop(0, groups, step, 0)

    def turn(q, carry):
        for i in range(8):
            m = table[pairs[1, q * 8 + i] * 128 + pairs[0, q * 8 + i]]
            out[q, 1, :, i : i + 1, :] = out[m // 8, 0, :, pl.ds(m % 8, 1), :]
        return carry

    lax.fori_loop(0, pair_count // 8, turn, 0)


def slot_sums(amplitudes, halo, blocks, ab, cd, live, pair_list, tiles_ab):
    pair_count, depth = halo.shape[1:]
    slots, width = blocks.shape[:2]
    anywhere = pl.BlockSpec(memory_space=pl.ANY)
    scalars = pl.BlockSpec(memory_space=pltpu.SMEM)
    return pl.pallas_call(
        slots_kernel,
        out_shape=jax.ShapeDtypeStruct((pair_count // 8, 2, tiles_ab, 8, width), jnp.float32),
        in_specs=[anywhere] * 3 + [scalars] * 4,
        out_specs=pl.BlockSpec(memory_space=pltpu.VMEM),
        scratch_shapes=[
            pltpu.VMEM((slots, pair_count, depth), jnp.float32),
            pltpu.VMEM((slots, width, depth), jnp.float32),
            pltpu.SemaphoreType.DMA((slots // GROUP,)),
            pltpu.SemaphoreType.DMA((slots // GROUP,)),
            pltpu.SMEM((128 * 128,), jnp.int32),
        ],
        compiler_params=pltpu.CompilerParams(vmem_limit_bytes=VMEM_BYTES),
    )(amplitudes, halo, blocks, ab, cd, live, pair_list)


def sum_kernel(sums, ladder, turned, bx, sz, bz, mine, send_x, recv_x, send_z, recv_z, send_r, recv_r):
    k, r, z, x = place()
    other_x = (z * 2 + 1 - x, r)
    zs = [((z + i) % 4 * 2 + x, r) for i in range(1, 4)]
    rows = [(k, (r + i) % 4) for i in range(1, 4)]
    greet([other_x] + zs + rows)

    def remote(src, dst, sent, received, device):
        return pltpu.make_async_remote_copy(
            src_ref=src, dst_ref=dst, send_sem=sent, recv_sem=received, device_id=device, device_id_type=MESH
        )

    steps = [(i, h) for h in (1, 0) for i in (2, 1, 3, 0)]
    over_x = {
        (i, h): remote(
            sums.at[(z + i) % 4 * 2 + 1 - x, h], bx.at[i, h], send_x.at[i, h], recv_x.at[i, h], other_x
        )
        for i, h in steps
    }
    over_z = {
        (i, h): remote(sz.at[i, h], bz.at[i, h], send_z.at[i, h], recv_z.at[i, h], zs[i - 1])
        for i, h in steps if i > 0
    }
    for step in steps[:WINDOW]:
        over_x[step].start()
    for j, (i, h) in enumerate(steps):
        over_x[i, h].wait_recv()
        if j + WINDOW < len(steps):
            over_x[steps[j + WINDOW]].start()
        total = bx[i, h] + sums[(z + i) % 4 * 2 + x, h]
        if i > 0:
            sz[i, h] = total
            over_z[i, h].start()
        else:
            mine[h] = total
    def finish(h):
        for i in (1, 3, 2):
            over_z[i, h].wait_recv()
        return mine[h] + bz[1, h] + bz[2, h] + bz[3, h]

    mine[1] = finish(1)
    parts = mine.at[1]

    def over_row(i):
        first = (r + i) % 4 * 3 // 2
        return [
            remote(
                parts.at[pl.ds(t * 6 + first, 2)], turned.at[r, t], send_r.at[i, t], recv_r.at[i, t], rows[i - 1]
            )
            for t in range(3)
        ]

    copies = [c for i in range(1, 4) for c in over_row(i)]
    for c in copies:
        c.start()
    own = r * 3 // 2
    for t in range(3):
        turned[r, t] = mine[1, pl.ds(t * 6 + own, 2)]
    ladder[...] = finish(0).reshape(ladder.shape)
    for i in range(1, 4):
        source = (r + 4 - i) % 4
        for t in range(3):
            remote(
                parts.at[pl.ds(0, 2)], turned.at[source, t], send_r.at[i, t], recv_r.at[i, t], rows[i - 1]
            ).wait_recv()
    for c in copies + list(over_x.values()) + list(over_z.values()):
        c.wait_send()


def sum_over_tile(sums):
    chunk = sums.shape[1:]
    vmem = pl.BlockSpec(memory_space=pltpu.VMEM)
    dma = pltpu.SemaphoreType.DMA
    return pl.pallas_call(
        sum_kernel,
        out_shape=(
            jax.ShapeDtypeStruct((3, 6) + chunk[2:], jnp.float32),
            jax.ShapeDtypeStruct((4, 3, 2) + chunk[2:], jnp.float32),
        ),
        in_specs=[vmem],
        out_specs=(vmem, vmem),
        scratch_shapes=[
            pltpu.VMEM((4,) + chunk, jnp.float32),
            pltpu.VMEM((4,) + chunk, jnp.float32),
            pltpu.VMEM((4,) + chunk, jnp.float32),
            pltpu.VMEM(chunk, jnp.float32),
            dma((4, 2)), dma((4, 2)), dma((4, 2)), dma((4, 2)), dma((4, 3)), dma((4, 3)),
        ],
        compiler_params=pltpu.CompilerParams(
            collective_id=1, has_side_effects=True, vmem_limit_bytes=16 * 1024 * 1024
        ),
    )(sums)


def shards_8x4(amplitudes, integrals, slot_ab, slot_cd, live_count, pair_list):
    halo = halo_of(amplitudes)
    sums = slot_sums(amplitudes, halo, integrals[0], slot_ab, slot_cd, live_count, pair_list.T, 18)
    ladder, turned = sum_over_tile(sums)
    local_pairs = ladder.shape[2]
    grid = jnp.transpose(ladder.reshape(3, 6, local_pairs, ATS, TS), (2, 0, 3, 1, 4)).reshape(local_pairs, 24, SLAB)
    other = turned.reshape(4, 3, 2, local_pairs, ATS, TS)
    other = jnp.transpose(other, (3, 2, 5, 0, 1, 4)).reshape(local_pairs, 2 * TS, SLAB)
    shift = lax.axis_index("row") % 2 * 8
    return grid + lax.dynamic_slice_in_dim(other, shift, 24, axis=1)


def solution(mesh):
    fast = mesh.shape["tile"] == 8 and mesh.shape["row"] == 4
    return jax.shard_map(
        shards_8x4 if fast else shards,
        mesh=mesh,
        in_specs=(
            P("tile", None, None),
            P("row", "tile", None, None),
            P("row", "tile"),
            P("row", "tile"),
            P("row", "tile"),
            P(),
        ),
        out_specs=P("tile", "row", None),
        check_vma=False,
    )
```
